32 devices in a mesh: grp: 8 (over y, x, core), head: 4 (over z).
Axes of the slice: x: 2, y: 2, z: 4, core: 2. Of those that a mesh axis runs over, the one named last changes fastest.
Arguments:
- new_keys: bfloat16 [4096, 16, 1024], P('grp', None, 'head'), may hold values from -8 to 8
- new_values: bfloat16 [4096, 16, 1024], P('grp', None, 'head'), may hold values from -6 to 6
- page_dest: int32 [4096], P('grp'), may hold values from 0 to 7, as said below
- page_slot: int32 [4096], P('grp'), may hold values from 0 to 511, as said below
- resident_keys: bfloat16 [1536, 16, 1024], P('grp', None, 'head'), may hold values from -8 to 8
- resident_values: bfloat16 [1536, 16, 1024], P('grp', None, 'head'), may hold values from -6 to 6
- queries: bfloat16 [16, 8192], P('grp', 'head'), may hold values from -11 to 11
- self_keys: bfloat16 [16, 1024], P('grp', 'head'), may hold values from -6 to 6
- self_values: bfloat16 [16, 1024], P('grp', 'head'), may hold values from -6 to 6
- context_len: int32 [16], P('grp'), may hold values from 1009 to 10240, as said below
- selected: int32 [16, 64], P('grp'), may hold values from 0 to 639, as said below
- out_weight: bfloat16 [8192, 3072], P('head'), may hold values from -0.0625 to 0.0625
Outputs:
- pool_keys: bfloat16 [4096, 16, 1024], P('grp', None, 'head')
- pool_values: bfloat16 [4096, 16, 1024], P('grp', None, 'head')
- slot_bounds: float32 [64, 5632], P('head', 'grp')
- projected: bfloat16 [16, 3072], P('grp', 'head')
The draws below stay inside these ranges and needn't reach their ends.
Inputs may be any that keep to these rules, and one draw needn't show every extreme that they name: `page_dest`: each device of grp sends at most 128 of its pages to one owner and exactly 128 to some owner; every owner receives 512 pages in all. `page_slot`: the pages that one owner receives take its slots 0 to 511 once each. ceil(context_len / 16) is at least 64 for every row and sums to 704 over the rows of one device of grp. `selected`: 64 distinct page numbers below ceil(context_len / 16) of the row; the row's last page is always among them.
All inputs are finite; a program needn't handle non-finite values.
Results may differ from the reference program's by a relative error of at most 0.0051.
Values may be sent and summed in bfloat16 or wider, within the bound.
No kernel may reach another device: no remote copies, remote signals or barrier semaphores. Data moves between devices by JAX's collectives and lax.ppermute only.
A program may use at most 128 MiB of HBM per device.

```python
import math
import jax
import jax.numpy as jnp
from jax import lax

HD = 128
KVH = 8
QH = 64
D_OUT = 3072
PAGE = 16
K_SEL = 64
NEW_DEV = 512
RES_DEV = 192
ROWS_DEV = 2
POOL = 704
ROWS = 16
GROUP_PAGES = 4096
RESIDENT = 1536
SLOTS = 5632
N_GRP = 8


def placement_lists(key):
    groups = N_GRP
    per_source = NEW_DEV
    capacity = 2 * per_source // groups
    remaining = per_source - capacity
    typical = remaining // (groups - 1)
    surplus = remaining - typical * (groups - 1)
    spread = max(0, min(typical - 1, capacity - 2 - typical))
    paired = (groups - 1) // 2
    others = typical + (jax.random.permutation(jax.random.fold_in(key, 1), groups - 1) < surplus).astype(jnp.int32)
    shifts = jax.random.randint(jax.random.fold_in(key, 2), (paired,), -spread, spread + 1).astype(jnp.int32)
    shuffled = jax.random.permutation(jax.random.fold_in(key, 3), groups - 1)
    others = others.at[shuffled[0:2 * paired:2]].add(shifts).at[shuffled[1:2 * paired:2]].add(-shifts)
    counts_out = jnp.concatenate([jnp.full((1,), capacity, jnp.int32), others.astype(jnp.int32)])
    counts_out = jnp.roll(counts_out, jax.random.randint(jax.random.fold_in(key, 4), (), 0, groups))
    limits = jnp.cumsum(counts_out)
    source_keys = jax.random.split(jax.random.fold_in(key, 5), groups)
    ranking = jax.vmap(lambda subkey: jax.random.permutation(subkey, per_source))(source_keys).astype(jnp.int32)
    offsets = jnp.sum((ranking[:, :, None] >= limits[None, None, :]).astype(jnp.int32), axis=2)
    owners = jax.random.permutation(jax.random.fold_in(key, 6), groups).astype(jnp.int32)
    sources = jnp.arange(groups, dtype=jnp.int32)[:, None]
    targets = owners[(sources + offsets) % groups].reshape(-1)
    everything = groups * per_source
    tiebreak = jax.random.permutation(jax.random.fold_in(key, 7), everything).astype(jnp.int32)
    ordering = jnp.argsort(targets * everything + tiebreak)
    position = jnp.zeros((everything,), jnp.int32).at[ordering].set(jnp.arange(everything, dtype=jnp.int32))
    return (targets.astype(jnp.int32), (position - targets * per_source).astype(jnp.int32))


def row_layout(key):
    owners_count = N_GRP
    rows_here = ROWS_DEV
    spare = POOL - rows_here * K_SEL

    def split_spare(subkey):
        cuts = jnp.sort(jax.random.permutation(subkey, spare + rows_here - 1)[:rows_here - 1]).astype(jnp.int32)
        edges = jnp.concatenate([jnp.full((1,), -1, jnp.int32), cuts, jnp.full((1,), spare + rows_here - 1, jnp.int32)])
        return edges[1:] - edges[:-1] - 1
    spares = jax.vmap(split_spare)(jax.random.split(jax.random.fold_in(key, 11), owners_count))
    tails = jax.random.randint(jax.random.fold_in(key, 12), (owners_count, rows_here), 1, PAGE + 1).astype(jnp.int32)
    chosen_owner = jax.random.randint(jax.random.fold_in(key, 13), (), 0, owners_count)
    chosen_row = jax.random.randint(jax.random.fold_in(key, 14), (), 0, rows_here)
    row_ids = jnp.arange(rows_here, dtype=jnp.int32)
    forced_spare = jnp.where(row_ids == chosen_row, spare, 0).astype(jnp.int32)
    forced_tail = jnp.where(row_ids == chosen_row, PAGE, jnp.where(row_ids == (chosen_row + 1) % rows_here, 1, tails[chosen_owner])).astype(jnp.int32)
    is_forced = (jnp.arange(owners_count, dtype=jnp.int32) == chosen_owner)[:, None]
    spares = jnp.where(is_forced, forced_spare[None, :], spares)
    tails = jnp.where(is_forced, forced_tail[None, :], tails)
    pages = K_SEL + spares
    lengths = (pages - 1) * PAGE + tails
    return (lengths.reshape(-1).astype(jnp.int32), pages.reshape(-1).astype(jnp.int32))


def query_common(key):
    return jnp.clip(jax.random.normal(jax.random.fold_in(key, 32), (ROWS, KVH, HD), jnp.float32), -4.0, 4.0)


def draw_page_dest(key, part):
    targets, places = placement_lists(key)
    return targets


def draw_page_slot(key, part):
    targets, places = placement_lists(key)
    return places


def draw_context_len(key, part):
    lengths, pages = row_layout(key)
    return lengths


def draw_selected(key, part):
    lengths, pages = row_layout(key)
    key = jax.random.fold_in(key, 21)
    ranking = jax.vmap(lambda subkey: jax.random.permutation(subkey, POOL))(jax.random.split(key, ROWS)).astype(jnp.int32)
    columns = jnp.arange(POOL, dtype=jnp.int32)[None, :]
    ranking = jnp.where(columns < pages[:, None], ranking, -1)
    ranking = jnp.where(columns == pages[:, None] - 1, POOL, ranking)
    picked = lax.top_k(ranking, K_SEL)[1]
    return picked.astype(jnp.int32)


def draw_new_keys(key, part):
    key = jax.random.fold_in(key, 51)
    noise = jnp.clip(jax.random.normal(key, (GROUP_PAGES, PAGE, KVH, HD), jnp.float32), -6.0, 6.0)
    return noise.reshape(GROUP_PAGES, PAGE, KVH * HD).astype(jnp.bfloat16)


def draw_resident_keys(key, part):
    key = jax.random.fold_in(key, 52)
    noise = jnp.clip(jax.random.normal(key, (RESIDENT, PAGE, KVH, HD), jnp.float32), -6.0, 6.0)
    return noise.reshape(RESIDENT, PAGE, KVH * HD).astype(jnp.bfloat16)


def draw_queries(key, part):
    common = query_common(key)
    key = jax.random.fold_in(key, 61)
    own_part = jnp.clip(jax.random.normal(key, (ROWS, KVH, QH // KVH, HD), jnp.float32), -4.0, 4.0)
    result = 0.8 * common[:, :, None, :] + 0.6 * own_part
    return result.reshape(ROWS, QH * HD).astype(jnp.bfloat16)


def draw_self_keys(key, part):
    common = query_common(key)
    key = jax.random.fold_in(key, 71)
    noise = jnp.clip(jax.random.normal(key, (ROWS, KVH, HD), jnp.float32), -4.0, 4.0)
    return (0.73 * common + 0.7 * noise).reshape(ROWS, KVH * HD).astype(jnp.bfloat16)


def steps_of(key, dims, pieces, low, largest):
    factor_of = 1.0
    for dim, parts in pieces:
        steps = jax.random.uniform(jax.random.fold_in(jax.random.fold_in(key, 6), dim), (parts,), jnp.float32, low / len(pieces), largest / len(pieces))
        factor_of = factor_of * jnp.repeat(jnp.exp(steps), dims[dim] // parts).reshape((-1,) + (1,) * (len(dims) - 1 - dim))
    return factor_of


def normal_values(stream_key, shape, scale, bound, shards=(), kind=jnp.bfloat16):
    values = scale * jax.random.normal(stream_key, shape, jnp.float32)
    if shards:
        values = values * steps_of(stream_key, shape, shards, -0.22, 0.18)
    return jnp.clip(values, -bound, bound).astype(kind)


def setup_inputs(seed: int = 0) -> dict:
    key_list = jax.random.split(jax.random.key(seed), 13)
    return {
        "new_keys": draw_new_keys(jax.random.fold_in(key_list[12], 71), 0),
        "new_values": normal_values(key_list[1], (GROUP_PAGES, PAGE, KVH * HD), 1.0, 6.0, ((0, 8), (2, 4))),
        "page_dest": draw_page_dest(jax.random.fold_in(key_list[12], 71), 0),
        "page_slot": draw_page_slot(jax.random.fold_in(key_list[12], 71), 0),
        "resident_keys": draw_resident_keys(jax.random.fold_in(key_list[12], 71), 0),
        "resident_values": normal_values(key_list[5], (RESIDENT, PAGE, KVH * HD), 1.0, 6.0, ((0, 8), (2, 4))),
        "queries": draw_queries(jax.random.fold_in(key_list[12], 71), 0),
        "self_keys": draw_self_keys(jax.random.fold_in(key_list[12], 71), 0),
        "self_values": normal_values(key_list[8], (ROWS, KVH * HD), 1.0, 6.0, ((0, 8), (1, 4))),
        "context_len": draw_context_len(jax.random.fold_in(key_list[12], 71), 0),
        "selected": draw_selected(jax.random.fold_in(key_list[12], 71), 0),
        "out_weight": normal_values(key_list[11], (QH * HD, D_OUT), (QH * HD) ** -0.5, 0.0625, ((0, 4),)),
    }


def reference(new_keys, new_values, page_dest, page_slot, resident_keys, resident_values, queries, self_keys, self_values, context_len, selected, out_weight):
    row_width = KVH * HD
    group_size = QH // KVH
    score_scale = 1.0 / math.sqrt(HD)
    targets = (page_dest * NEW_DEV + page_slot).astype(jnp.int32)
    pool_keys = jnp.zeros((GROUP_PAGES, PAGE, row_width), new_keys.dtype).at[targets].set(new_keys)
    pool_values = jnp.zeros((GROUP_PAGES, PAGE, row_width), new_values.dtype).at[targets].set(new_values)
    cache_keys = jnp.concatenate([resident_keys.reshape(N_GRP, RES_DEV, PAGE, row_width), pool_keys.reshape(N_GRP, NEW_DEV, PAGE, row_width)], axis=1)
    cache_values = jnp.concatenate([resident_values.reshape(N_GRP, RES_DEV, PAGE, row_width), pool_values.reshape(N_GRP, NEW_DEV, PAGE, row_width)], axis=1)
    per_owner = (cache_keys, cache_values, queries.reshape(N_GRP, ROWS_DEV, QH * HD), self_keys.reshape(N_GRP, ROWS_DEV, row_width), self_values.reshape(N_GRP, ROWS_DEV, row_width), context_len.reshape(N_GRP, ROWS_DEV), selected.reshape(N_GRP, ROWS_DEV, K_SEL))

    def owner_step(inputs):
        owner_keys, owner_values, owner_queries, owner_self_keys, owner_self_values, owner_lengths, owner_selected = inputs
        page_counts = (owner_lengths + PAGE - 1) // PAGE
        row_end = jnp.cumsum(page_counts).astype(jnp.int32)
        row_start = (row_end - page_counts).astype(jnp.int32)
        slot_ids = jnp.arange(POOL, dtype=jnp.int32)
        owner_row = lax.optimization_barrier(jnp.sum((slot_ids[:, None] >= row_end[None, :]).astype(jnp.int32), axis=1))
        lowest = lax.optimization_barrier(jnp.min(owner_keys, axis=1)).astype(jnp.float32).reshape(POOL, KVH, 1, HD)
        highest = lax.optimization_barrier(jnp.max(owner_keys, axis=1)).astype(jnp.float32).reshape(POOL, KVH, 1, HD)
        per_slot = jnp.take(owner_queries, owner_row, axis=0).astype(jnp.float32).reshape(POOL, KVH, group_size, HD)
        criticality = lax.optimization_barrier(jnp.sum(jnp.maximum(per_slot * highest, per_slot * lowest), axis=3)) * score_scale
        criticality = criticality.reshape(POOL, QH).T
        page_slots = (row_start[:, None] + owner_selected).astype(jnp.int32)
        picked_keys = jnp.take(owner_keys, page_slots, axis=0).reshape(ROWS_DEV, K_SEL * PAGE, KVH, HD).astype(jnp.float32)
        picked_values = jnp.take(owner_values, page_slots, axis=0).reshape(ROWS_DEV, K_SEL * PAGE, KVH, HD).astype(jnp.float32)
        query_heads = owner_queries.reshape(ROWS_DEV, KVH, group_size, HD).astype(jnp.float32)
        scores = jnp.einsum('rhgd,rthd->rhgt', query_heads, picked_keys) * score_scale
        self_scores = jnp.einsum('rhgd,rhd->rhg', query_heads, owner_self_keys.reshape(ROWS_DEV, KVH, HD).astype(jnp.float32)) * score_scale
        within = jnp.arange(PAGE, dtype=jnp.int32)
        live_tokens = (owner_selected[:, :, None] * PAGE + within[None, None, :] < owner_lengths[:, None, None]).reshape(ROWS_DEV, K_SEL * PAGE)
        live_mask = live_tokens[:, None, None, :]
        scores = jnp.where(live_mask, scores, -1e+30)
        row_top = jnp.maximum(lax.optimization_barrier(jnp.max(scores, axis=3)), self_scores)
        weights = jnp.where(live_mask, jnp.exp(scores - row_top[..., None]), 0.0)
        self_weight = jnp.exp(self_scores - row_top)
        total_weight = lax.optimization_barrier(jnp.sum(weights, axis=3)) + self_weight
        rounded = lax.optimization_barrier(weights.astype(jnp.bfloat16)).astype(jnp.float32)
        self_rounded = lax.optimization_barrier(self_weight.astype(jnp.bfloat16)).astype(jnp.float32)
        blended = jnp.einsum('rhgt,rthd->rhgd', rounded, picked_values)
        blended = blended + self_rounded[..., None] * owner_self_values.reshape(ROWS_DEV, KVH, HD).astype(jnp.float32)[:, :, None, :]
        attended = (blended / total_weight[..., None]).reshape(ROWS_DEV, QH * HD).astype(jnp.bfloat16)
        return (criticality, attended)
    criticality, attended = lax.map(owner_step, per_owner)
    slot_bounds = jnp.transpose(criticality, (1, 0, 2)).reshape(QH, SLOTS)
    projected = jnp.dot(attended.reshape(ROWS, QH * HD), out_weight, preferred_element_type=jnp.float32).astype(jnp.bfloat16)
    return (pool_keys, pool_values, slot_bounds, projected)
```

```python
import functools
import math

import jax
import jax.numpy as jnp
from jax import lax
from jax.experimental import pallas as pl
from jax.experimental.pallas import tpu as pltpu
from jax.sharding import PartitionSpec as P

HD = 128
CORES = 2
HBM = pl.BlockSpec(memory_space=pltpu.HBM)
SMEM = pl.BlockSpec(memory_space=pltpu.SMEM)
VMEM = pl.BlockSpec(memory_space=pltpu.VMEM)
VMEM_LIMIT = 48 << 20


def params(**kw):
    return pltpu.CompilerParams(vmem_limit_bytes=VMEM_LIMIT, **kw)


def copy(src, dst, sem):
    return pltpu.make_async_copy(src, dst, sem)


def invert(masks, payloads, width):
    ranks = jnp.where(masks, jnp.cumsum(masks.astype(jnp.int32), axis=1) - 1, -1)
    places = jnp.arange(width, dtype=jnp.int32)
    hits = ranks[:, None, :] == places[None, :, None]
    return jnp.sum(jnp.where(hits, payloads[:, None, :] + 1, 0), axis=2) - 1


def pack_pages(info, lists, offset, count, own_k, own_v, sib_k, sib_v):
    shifts = lists.shape[0]
    per_source = own_k.shape[0]
    page = own_k.shape[1:]

    def kernel(info_ref, list_ref, ok, ov, sk, sv, *rest):
        outs, (buf, sems, out_sems) = rest[:shifts], rest[shifts:]
        core = info_ref[0]

        def gather(own, sib):
            base = core * per_source

            for s in range(shifts):

                def body(j, carry, s=s):
                    i = jnp.maximum(list_ref[s, offset + j], 0)
                    local = i - base
                    is_own = (local >= 0) & (local < per_source)
                    row = jnp.where(i >= per_source, i - per_source, i)

                    @pl.when(is_own)
                    def _():
                        copy(own.at[row], buf.at[s, j], sems.at[s]).start()

                    @pl.when(jnp.logical_not(is_own))
                    def _():
                        copy(sib.at[row], buf.at[s, j], sems.at[s]).start()

                    return carry

                lax.fori_loop(0, count, body, 0)

        @pl.when(core == 0)
        def _():
            gather(ok, sk)

        @pl.when(core != 0)
        def _():
            gather(ov, sv)

        for s in range(shifts):
            copy(buf.at[s], buf.at[s], sems.at[s]).wait()
            copy(buf.at[s], outs[s], out_sems.at[s]).start()
        for s in range(shifts):
            copy(buf.at[s], outs[s], out_sems.at[s]).wait()

    return pl.pallas_call(
        kernel,
        out_shape=[jax.ShapeDtypeStruct((count,) + page, own_k.dtype)] * shifts,
        in_specs=[SMEM, SMEM, HBM, HBM, HBM, HBM],
        out_specs=[HBM] * shifts,
        scratch_shapes=[
            pltpu.VMEM((shifts, count) + page, own_k.dtype),
            pltpu.SemaphoreType.DMA((shifts,)),
            pltpu.SemaphoreType.DMA((shifts,)),
        ],
        compiler_params=params(),
        name="pack_pages",
    )(info, lists, own_k, own_v, sib_k, sib_v)


def pack_local(info, to_sib, own_k, own_v):
    count = to_sib.shape[1]
    page = own_k.shape[1:]

    def kernel(info_ref, list_ref, ok, ov, out, buf, sem, out_sem):
        core = info_ref[0]

        def gather(own):
            def body(j, carry):
                copy(own.at[jnp.maximum(list_ref[0, j], 0)], buf.at[j], sem).start()
                return carry

            lax.fori_loop(0, count, body, 0)

        @pl.when(core == 0)
        def _():
            gather(ok)

        @pl.when(core != 0)
        def _():
            gather(ov)

        copy(buf, buf, sem).wait()
        done = copy(buf, out, out_sem)
        done.start()
        done.wait()

    return pl.pallas_call(
        kernel,
        out_shape=jax.ShapeDtypeStruct((count,) + page, own_k.dtype),
        in_specs=[SMEM, SMEM, HBM, HBM],
        out_specs=HBM,
        scratch_shapes=[
            pltpu.VMEM((count,) + page, own_k.dtype),
            pltpu.SemaphoreType.DMA,
            pltpu.SemaphoreType.DMA,
        ],
        compiler_params=params(),
        name="pack_local",
    )(info, to_sib, own_k, own_v)


def settle_local(info, own_list, sib_list, own_k, own_v, sib_k, sib_v, crossed):
    count = own_list.shape[1]
    per_source = own_k.shape[0]
    page = own_k.shape[1:]

    def kernel(info_ref, own_ref, sib_ref, ok, ov, sk, sv, cross, pk, pv, kb, vb, sem, sem2, osem):
        core = info_ref[0]

        def gather_own(j, n):
            v = own_ref[0, j]

            @pl.when(v >= 0)
            def _():
                row = v // per_source
                copy(ok.at[row], kb.at[j], sem).start()
                copy(ov.at[row], vb.at[j], sem).start()

            return n + jnp.where(v >= 0, 2, 0)

        n_own = lax.fori_loop(0, count, gather_own, 0)

        def gather_sib(role, role_buf, other_buf):
            bulk = copy(cross, other_buf.at[pl.ds(count, count)], sem2)
            bulk.start()

            def body(j, n):
                v = sib_ref[0, j]

                @pl.when(v >= 0)
                def _():
                    copy(role.at[v // per_source], role_buf.at[count + j], sem).start()

                return n + jnp.where(v >= 0, 1, 0)

            n_sib = lax.fori_loop(0, count, body, 0)

            def drain(j, carry):
                copy(role.at[0], role_buf.at[0], sem).wait()
                return carry

            lax.fori_loop(0, n_own + n_sib, drain, 0)
            bulk.wait()

        @pl.when(core == 0)
        def _():
            gather_sib(sk, kb, vb)

        @pl.when(core != 0)
        def _():
            gather_sib(sv, vb, kb)

        def scatter(ref, base):
            def body(j, n):
                v = ref[0, j]

                @pl.when(v >= 0)
                def _():
                    slot = v - (v // per_source) * per_source
                    copy(kb.at[base + j], pk.at[slot], osem).start()
                    copy(vb.at[base + j], pv.at[slot], osem).start()

                return n + jnp.where(v >= 0, 2, 0)

            return lax.fori_loop(0, count, body, 0)

        total = scatter(own_ref, 0) + scatter(sib_ref, count)

        def drain_out(j, carry):
            copy(kb.at[0], pk.at[0], osem).wait()
            return carry

        lax.fori_loop(0, total, drain_out, 0)

    shape = jax.ShapeDtypeStruct(own_k.shape, own_k.dtype)
    return pl.pallas_call(
        kernel,
        out_shape=[shape, shape],
        in_specs=[SMEM, SMEM, SMEM] + [HBM] * 5,
        out_specs=[HBM, HBM],
        scratch_shapes=[
            pltpu.VMEM((2 * count,) + page, own_k.dtype),
            pltpu.VMEM((2 * count,) + page, own_k.dtype),
            pltpu.SemaphoreType.DMA,
            pltpu.SemaphoreType.DMA,
            pltpu.SemaphoreType.DMA,
        ],
        compiler_params=params(),
        name="settle_local",
    )(info, own_list, sib_list, own_k, own_v, sib_k, sib_v, crossed)


def settle_pages(info, arrivals, offset, direct, swapped, pool_k, pool_v):
    shifts = len(direct)
    count = direct[0].shape[0]
    per_source = pool_k.shape[0]
    page = pool_k.shape[1:]

    def kernel(info_ref, arr_ref, *rest):
        d_refs, w_refs = rest[:shifts], rest[shifts : 2 * shifts]
        pk, pv, db, wb, sems, osem = rest[2 * shifts + 2 :]
        core = info_ref[0]
        low = core * per_source
        for s in range(shifts):
            copy(d_refs[s], db.at[s], sems.at[s, 0]).start()
            copy(w_refs[s], wb.at[s], sems.at[s, 1]).start()

        def scatter(direct_pool, swapped_pool):
            total = 0
            for s in range(shifts):
                copy(d_refs[s], db.at[s], sems.at[s, 0]).wait()
                copy(w_refs[s], wb.at[s], sems.at[s, 1]).wait()

                def body(j, n, s=s):
                    slot = arr_ref[s, offset + j] - low
                    mine = (slot >= 0) & (slot < per_source)

                    @pl.when(mine)
                    def _():
                        copy(db.at[s, j], direct_pool.at[slot], osem).start()
                        copy(wb.at[s, j], swapped_pool.at[slot], osem).start()

                    return n + jnp.where(mine, 2, 0)

                total = lax.fori_loop(0, count, body, total)

            def drain(j, carry):
                copy(db.at[0, 0], direct_pool.at[0], osem).wait()
                return carry

            lax.fori_loop(0, total, drain, 0)

        @pl.when(core == 0)
        def _():
            scatter(pk, pv)

        @pl.when(core != 0)
        def _():
            scatter(pv, pk)

    shape = jax.ShapeDtypeStruct(pool_k.shape, pool_k.dtype)
    return pl.pallas_call(
        kernel,
        out_shape=[shape, shape],
        in_specs=[SMEM, SMEM] + [HBM] * (2 * shifts + 2),
        out_specs=[HBM, HBM],
        input_output_aliases={2 + 2 * shifts: 0, 3 + 2 * shifts: 1},
        scratch_shapes=[
            pltpu.VMEM((shifts, count) + page, pool_k.dtype),
            pltpu.VMEM((shifts, count) + page, pool_k.dtype),
            pltpu.SemaphoreType.DMA((shifts, 2)),
            pltpu.SemaphoreType.DMA,
        ],
        compiler_params=params(),
        name="settle_pages",
    )(info, arrivals, *direct, *swapped, pool_k, pool_v)


def bounds_of(row_of, queries, pages, block):
    n_pages, page_rows, width = pages.shape
    rows = queries.shape[0]
    kv_local = width // HD
    heads = queries.shape[1] // HD
    group = heads // kv_local
    scale = 1.0 / math.sqrt(HD)

    def kernel(row_ref, q_ref, page_ref, out_ref):
        x = page_ref[...]
        low = jnp.min(x, axis=1)
        high = jnp.max(x, axis=1)
        owner = row_ref[...]
        for h in range(kv_local):
            part = slice(h * HD, (h + 1) * HD)
            result = jnp.zeros((group, block), jnp.float32)
            for r in range(rows):
                q = q_ref[r, h * group : (h + 1) * group, :]
                zero = jnp.zeros_like(q)
                dims = (((1,), (1,)), ((), ()))
                both = lax.dot_general(
                    jnp.maximum(q, zero), high[:, part], dims, preferred_element_type=jnp.float32
                ) + lax.dot_general(
                    jnp.minimum(q, zero), low[:, part], dims, preferred_element_type=jnp.float32
                )
                result = jnp.where(owner == r, both, result)
            out_ref[h * group : (h + 1) * group, :] = result * scale

    return pl.pallas_call(
        kernel,
        grid=(n_pages // block,),
        out_shape=jax.ShapeDtypeStruct((heads, n_pages), jnp.float32),
        in_specs=[
            pl.BlockSpec((1, block), lambda i: (0, i)),
            pl.BlockSpec((rows, heads, HD), lambda i: (0, 0, 0)),
            pl.BlockSpec((block, page_rows, width), lambda i: (i, 0, 0)),
        ],
        out_specs=pl.BlockSpec((heads, block), lambda i: (0, i)),
        compiler_params=params(),
        name="bounds",
    )(row_of, queries.reshape(rows, heads, HD), pages)


def attend(page_slots, live, queries, self_keys, self_values, res_k, res_v, pool_k, pool_v):
    rows, k_sel = page_slots.shape
    res_count, page_rows, width = res_k.shape
    kv_local = width // HD
    heads = queries.shape[1] // HD
    group = heads // kv_local
    tokens = k_sel * page_rows
    scale = 1.0 / math.sqrt(HD)

    def kernel(slot_ref, live_ref, q_ref, sk_ref, sv_ref, rk, rv, pk, pv, out_ref, kb, vb, sems):
        for r in range(rows):

            def body(j, carry, r=r):
                slot = slot_ref[r, j]

                @pl.when(slot < res_count)
                def _():
                    copy(rk.at[slot], kb.at[r, j], sems.at[r, 0]).start()
                    copy(rv.at[slot], vb.at[r, j], sems.at[r, 1]).start()

                @pl.when(slot >= res_count)
                def _():
                    copy(pk.at[slot - res_count], kb.at[r, j], sems.at[r, 0]).start()
                    copy(pv.at[slot - res_count], vb.at[r, j], sems.at[r, 1]).start()

                return carry

            lax.fori_loop(0, k_sel, body, 0)
        for r in range(rows):
            copy(kb.at[r], kb.at[r], sems.at[r, 0]).wait()
            copy(vb.at[r], vb.at[r], sems.at[r, 1]).wait()
            alive = live_ref[r : r + 1, :] > 0
            for h in range(kv_local):
                part = slice(h * HD, (h + 1) * HD)
                here = slice(h * group, (h + 1) * group)
                q = q_ref[r, here, :]
                keys = kb[r, :, :, part].reshape(tokens, HD)
                values = vb[r, :, :, part].reshape(tokens, HD)
                scores = (
                    lax.dot_general(
                        q, keys, (((1,), (1,)), ((), ())), preferred_element_type=jnp.float32
                    )
                    * scale
                )
                scores = jnp.where(alive, scores, -1e30)
                self_key = sk_ref[r : r + 1, part].astype(jnp.float32)
                self_score = (
                    jnp.sum(q.astype(jnp.float32) * self_key, axis=1, keepdims=True) * scale
                )
                top = jnp.maximum(jnp.max(scores, axis=1, keepdims=True), self_score)
                weights = jnp.where(alive, jnp.exp(scores - top), 0.0)
                self_weight = jnp.exp(self_score - top)
                total = jnp.sum(weights, axis=1, keepdims=True) + self_weight
                mixed = lax.dot_general(
                    weights.astype(jnp.bfloat16),
                    values,
                    (((1,), (0,)), ((), ())),
                    preferred_element_type=jnp.float32,
                )
                self_rounded = self_weight.astype(jnp.bfloat16).astype(jnp.float32)
                mixed = mixed + self_rounded * sv_ref[r : r + 1, part].astype(jnp.float32)
                out_ref[r, here, :] = (mixed / total).astype(jnp.bfloat16)

    return pl.pallas_call(
        kernel,
        out_shape=jax.ShapeDtypeStruct((rows, heads, HD), jnp.bfloat16),
        in_specs=[SMEM, VMEM, VMEM, VMEM, VMEM, HBM, HBM, HBM, HBM],
        out_specs=VMEM,
        scratch_shapes=[
            pltpu.VMEM((rows, k_sel, page_rows, width), jnp.bfloat16),
            pltpu.VMEM((rows, k_sel, page_rows, width), jnp.bfloat16),
            pltpu.SemaphoreType.DMA((rows, 2)),
        ],
        compiler_params=params(),
        name="attend",
    )(
        page_slots,
        live,
        queries.reshape(rows, heads, HD),
        self_keys,
        self_values,
        res_k,
        res_v,
        pool_k,
        pool_v,
    )


def project(attended, out_weight):
    ranks = lax.axis_size("head")
    here = lax.axis_index("head")
    partial = jnp.dot(attended, out_weight, preferred_element_type=jnp.float32)
    columns = partial.shape[1] // ranks

    def piece(owner):
        return lax.dynamic_slice_in_dim(partial, owner * columns, columns, 1)

    total = piece(here)
    for s in range(1, ranks):
        pairs = [(k, (k + s) % ranks) for k in range(ranks)]
        total = total + lax.ppermute(piece((here + s) % ranks), "head", pairs)
    return total.astype(jnp.bfloat16)


def chunks_of(total, unit):
    sizes = []
    left = total
    for part in (2 * unit, 4 * unit, 4 * unit, 4 * unit):
        if left > part + unit:
            sizes.append(part)
            left -= part
    if left > 2 * unit:
        sizes.append(left - unit)
        left = unit
    sizes.append(left)
    return sizes


def on_device(
    new_keys,
    new_values,
    page_dest,
    page_slot,
    resident_keys,
    resident_values,
    queries,
    self_keys,
    self_values,
    context_len,
    selected,
    out_weight,
):
    groups = lax.axis_size("grp")
    chips = groups // CORES
    me = lax.axis_index("grp")
    chip, core = me // CORES, me % CORES
    per_source, page_rows = new_keys.shape[:2]
    res_count = resident_keys.shape[0]
    rows_here = queries.shape[0]
    pair_cap = 2 * per_source // groups
    cap = CORES * CORES * pair_cap
    unit = cap // 16

    def permute(x, shift):
        return lax.ppermute(x, "grp", [(i, i ^ shift) for i in range(groups)])

    sib_keys = lax.ppermute(new_keys, "grp", [(i, i ^ 1) for i in range(groups) if i & 1])
    sib_values = lax.ppermute(new_values, "grp", [(i, i ^ 1) for i in range(groups) if not i & 1])

    everyone = lax.all_gather(jnp.stack([page_dest, page_slot]), "grp")
    dest = everyone[:, 0].reshape(chips, CORES * per_source)
    slot = everyone[:, 1].reshape(chips, CORES * per_source)
    dest_chip = dest // CORES
    chip_ids = jnp.arange(chips, dtype=jnp.int32)
    counts = jnp.sum((dest_chip[:, :, None] == chip_ids).astype(jnp.int32), axis=1)
    away = jnp.where(chip_ids[:, None] == chip_ids[None, :], 0, counts)
    needed = jnp.max(away)

    shifts = jnp.arange(1, chips, dtype=jnp.int32)
    partners = chip ^ shifts
    my_dest = dest[chip]
    my_slot = slot[chip]
    ids = jnp.arange(CORES * per_source, dtype=jnp.int32)
    sends = invert(
        (my_dest // CORES)[None, :] == partners[:, None],
        jnp.broadcast_to(ids, (chips - 1, ids.shape[0])),
        cap,
    )
    from_dest = jnp.take(dest, partners, axis=0)
    arrivals = invert(
        from_dest // CORES == chip,
        (from_dest % CORES) * per_source + jnp.take(slot, partners, axis=0),
        cap,
    )
    sib = me ^ 1
    sib_dest = lax.dynamic_index_in_dim(everyone, sib, 0, keepdims=False)
    own_ids = jnp.arange(per_source, dtype=jnp.int32)
    locals_ = invert(
        jnp.stack([page_dest == sib, page_dest == me, sib_dest[0] == me]),
        jnp.stack([own_ids, own_ids * per_source + page_slot, own_ids * per_source + sib_dest[1]]),
        pair_cap,
    )
    to_sib, from_own, from_sib = locals_[0:1], locals_[1:2], locals_[2:3]
    info = core.reshape(1)

    page_counts = (context_len + page_rows - 1) // page_rows
    row_end = jnp.cumsum(page_counts)
    row_start = row_end - page_counts
    slot_ids = jnp.arange(res_count + per_source, dtype=jnp.int32)
    owner_row = jnp.sum((slot_ids[None, :] >= row_end[:, None]).astype(jnp.int32), axis=0)[None]
    page_slots = row_start[:, None] + selected
    within = jnp.arange(page_rows, dtype=jnp.int32)
    live = (
        (selected[:, :, None] * page_rows + within[None, None, :] < context_len[:, None, None])
        .astype(jnp.int32)
        .reshape(rows_here, -1)
    )
    res_bounds = bounds_of(owner_row[:, :res_count], queries, resident_keys, res_count)

    def run(total):
        def branch(ops):
            sib_keys, sib_values, sends, arrivals = ops
            crossed = permute(pack_local(info, to_sib, new_keys, new_values), 1)
            pool_k, pool_v = settle_local(
                info, from_own, from_sib, new_keys, new_values, sib_keys, sib_values, crossed
            )
            offset = 0
            for size in chunks_of(total, unit):
                packed = pack_pages(
                    info, sends, offset, size, new_keys, new_values, sib_keys, sib_values
                )
                direct = [permute(x, (s + 1) * CORES) for s, x in enumerate(packed)]
                swapped = [permute(x, 1) for x in direct]
                pool_k, pool_v = settle_pages(
                    info, arrivals, offset, direct, swapped, pool_k, pool_v
                )
                offset += size
            pool_bounds = bounds_of(
                owner_row[:, res_count:], queries, pool_k, min(128, per_source)
            )
            attended = attend(
                page_slots,
                live,
                queries,
                self_keys,
                self_values,
                resident_keys,
                resident_values,
                pool_k,
                pool_v,
            )
            projected = project(attended.reshape(rows_here, -1), out_weight)
            return pool_k, pool_v, pool_bounds, projected

        return branch

    smallest = 7 if chips <= 4 else 16
    totals = [unit * k for k in range(smallest, 17)]
    which = jnp.clip((needed + unit - 1) // unit - smallest, 0, len(totals) - 1)
    pool_k, pool_v, pool_bounds, projected = lax.switch(
        which, [run(t) for t in totals], (sib_keys, sib_values, sends, arrivals)
    ) if len(totals) > 1 else run(totals[0])((sib_keys, sib_values, sends, arrivals))
    return pool_k, pool_v, jnp.concatenate([res_bounds, pool_bounds], axis=1), projected


def solution(mesh):
    in_specs = (
        P("grp", None, "head"),
        P("grp", None, "head"),
        P("grp"),
        P("grp"),
        P("grp", None, "head"),
        P("grp", None, "head"),
        P("grp", "head"),
        P("grp", "head"),
        P("grp", "head"),
        P("grp"),
        P("grp", None),
        P("head", None),
    )
    out_specs = (P("grp", None, "head"), P("grp", None, "head"), P("head", "grp"), P("grp", "head"))
    return jax.shard_map(
        on_device, mesh=mesh, in_specs=in_specs, out_specs=out_specs, check_vma=False
    )
```

```python
import functools
import math

import jax
import jax.numpy as jnp
from jax import lax
from jax.experimental import pallas as pl
from jax.experimental.pallas import tpu as pltpu
from jax.sharding import PartitionSpec as P

HD = 128
CORES = 2
ANY = pl.BlockSpec(memory_space=pl.ANY)
SMEM = pl.BlockSpec(memory_space=pltpu.SMEM)
VMEM = pl.BlockSpec(memory_space=pltpu.VMEM)
VMEM_LIMIT = 60 << 20


def params(**kw):
    return pltpu.CompilerParams(vmem_limit_bytes=VMEM_LIMIT, **kw)


def cost(size):
    return pl.CostEstimate(flops=0, bytes_accessed=size // 64, transcendentals=0)


def copy(src, dst, sem):
    return pltpu.make_async_copy(src, dst, sem)


def invert(marks, payloads, width):
    rows, size = marks.shape
    padded = -(-rows // 8) * 8
    marks = jnp.pad(marks.astype(jnp.int32), ((0, padded - rows), (0, 0)))
    payloads = jnp.pad(payloads, ((0, padded - rows), (0, 0)))

    def kernel(mark_ref, payload_ref, out_ref):
        marked = mark_ref[...]
        upto = (
            lax.broadcasted_iota(jnp.int32, (size, size), 0)
            <= lax.broadcasted_iota(jnp.int32, (size, size), 1)
        ).astype(jnp.float32)
        ranks = jnp.dot(
            marked.astype(jnp.float32).astype(jnp.bfloat16),
            upto.astype(jnp.bfloat16),
            preferred_element_type=jnp.float32,
        )
        ranks = jnp.where(marked > 0, ranks - 1.0, -1.0).astype(jnp.int32)
        places = lax.broadcasted_iota(jnp.int32, (width, size), 0)
        parts = lax.broadcasted_iota(jnp.int32, (8, size), 0)
        for t in range(rows):
            hits = (ranks[t : t + 1, :] == places).astype(jnp.float32).astype(jnp.bfloat16)
            value = payload_ref[t : t + 1, :]
            pieces = jnp.where(parts < 3, (value >> (7 * jnp.minimum(parts, 2))) & 127, 1)
            found = lax.dot_general(
                pieces.astype(jnp.float32).astype(jnp.bfloat16),
                hits,
                (((1,), (1,)), ((), ())),
                preferred_element_type=jnp.float32,
            ).astype(jnp.int32)
            whole = found[0:1] + found[1:2] * 128 + found[2:3] * 16384
            out_ref[t : t + 1, :] = jnp.where(found[3:4] > 0, whole, -1)

    return pl.pallas_call(
        kernel,
        out_shape=jax.ShapeDtypeStruct((rows, width), jnp.int32),
        in_specs=[VMEM, VMEM],
        out_specs=VMEM,
        compiler_params=params(),
        name="invert",
    )(marks, payloads)


def pack_pages(core, starts, lists, count, own_k, own_v, sib=None):
    shifts, width = lists.shape
    per_source = own_k.shape[0]
    page = own_k.shape[1:]
    sibs = () if sib is None else sib

    def kernel(core_ref, start_ref, list_ref, ok, ov, *rest):
        sib_refs, rest = rest[: len(sibs)], rest[len(sibs) :]
        outs, (buf, sems, out_sems) = rest[:shifts], rest[shifts:]

        def gather(own, other):
            for s in range(shifts):
                start = start_ref[s]

                def body(j, carry, s=s, start=start):
                    i = jnp.maximum(list_ref[s, jnp.minimum(start + j, width - 1)], 0)
                    if other is None:
                        copy(own.at[jnp.minimum(i, per_source - 1)], buf.at[s, j], sems.at[s]).start()
                    else:

                        @pl.when(i < per_source)
                        def _():
                            copy(own.at[i], buf.at[s, j], sems.at[s]).start()

                        @pl.when(i >= per_source)
                        def _():
                            copy(other.at[i - per_source], buf.at[s, j], sems.at[s]).start()

                    return carry

                lax.fori_loop(0, count, body, 0, unroll=4)

        @pl.when(core_ref[0] == 0)
        def _():
            gather(ok, sib_refs[0] if sibs else None)

        @pl.when(core_ref[0] != 0)
        def _():
            gather(ov, sib_refs[1] if sibs else None)

        for s in range(shifts):
            copy(buf.at[s], buf.at[s], sems.at[s]).wait()
            copy(buf.at[s], outs[s], out_sems.at[s]).start()
        for s in range(shifts):
            copy(buf.at[s], outs[s], out_sems.at[s]).wait()

    return pl.pallas_call(
        kernel,
        out_shape=[jax.ShapeDtypeStruct((count,) + page, own_k.dtype)] * shifts,
        in_specs=[SMEM, SMEM, SMEM, ANY, ANY] + [ANY] * len(sibs),
        out_specs=[ANY] * shifts,
        scratch_shapes=[
            pltpu.VMEM((shifts, count) + page, own_k.dtype),
            pltpu.SemaphoreType.DMA((shifts,)),
            pltpu.SemaphoreType.DMA((shifts,)),
        ],
        compiler_params=params(),
        cost_estimate=cost(shifts * count * page[0] * page[1] * 8),
        name="pack_pages",
    )(core, starts, lists, own_k, own_v, *sibs)


def settle_local(lists, own, sib, pools):
    count = lists.shape[1]
    per_source = own[0].shape[0]
    page = own[0].shape[1:]

    def kernel(list_ref, *rest):
        sources = (rest[0:2], rest[2:4])
        pk, pv, buf, sem, osem = rest[6:]
        targets = (pk, pv)

        def each(f):
            total = 0
            for who in range(2):

                def body(j, n, who=who):
                    v = list_ref[who, j]

                    @pl.when(v >= 0)
                    def _():
                        f(who, j, v // per_source, v % per_source)

                    return n + jnp.where(v >= 0, 2, 0)

                total = lax.fori_loop(0, count, body, total, unroll=2)
            return total

        def gather(who, j, row, slot):
            for kind in range(2):
                copy(sources[who][kind].at[row], buf.at[kind, who, j], sem).start()

        def scatter(who, j, row, slot):
            for kind in range(2):
                copy(buf.at[kind, who, j], targets[kind].at[slot], osem).start()

        def drain(a_sem):
            def body(j, carry):
                copy(buf.at[0, 0, 0], pk.at[0], a_sem).wait()
                return carry

            return body

        lax.fori_loop(0, each(gather), drain(sem), 0)
        lax.fori_loop(0, each(scatter), drain(osem), 0)

    shape = jax.ShapeDtypeStruct(own[0].shape, own[0].dtype)
    return pl.pallas_call(
        kernel,
        out_shape=[shape, shape],
        in_specs=[SMEM] + [ANY] * 6,
        out_specs=[ANY, ANY],
        input_output_aliases={5: 0, 6: 1},
        scratch_shapes=[
            pltpu.VMEM((2, 2, count) + page, own[0].dtype),
            pltpu.SemaphoreType.DMA,
            pltpu.SemaphoreType.DMA,
        ],
        compiler_params=params(),
        cost_estimate=cost(count * page[0] * page[1] * 32),
        name="settle_local",
    )(lists, *own, *sib, *pools)


def settle_pages(core, spans, lists, direct, swapped, per_source, pools=()):
    shifts = len(direct)
    count = direct[0].shape[0]
    page = direct[0].shape[1:]
    width = lists.shape[1]

    def kernel(core_ref, span_ref, list_ref, *rest):
        arrived = (rest[:shifts], rest[shifts : 2 * shifts])
        pk, pv, buf, sems, osem = rest[2 * shifts + len(pools) :]
        low = core_ref[0] * per_source
        for k in range(2):
            for s in range(shifts):
                copy(arrived[k][s], buf.at[k, s], sems.at[k, s]).start()

        def scatter(targets):
            total = 0
            for s in range(shifts):
                for k in range(2):
                    copy(arrived[k][s], buf.at[k, s], sems.at[k, s]).wait()
                    row = k * shifts + s
                    start, limit = span_ref[row, 0], span_ref[row, 1]

                    def body(j, n, s=s, k=k, row=row, start=start, limit=limit):
                        place = start + j
                        slot = list_ref[row, jnp.minimum(place, width - 1)] - low
                        mine = (slot >= 0) & (slot < per_source) & (place < limit)

                        @pl.when(mine)
                        def _():
                            copy(buf.at[k, s, j], targets[k].at[slot], osem).start()

                        return n + jnp.where(mine, 1, 0)

                    total = lax.fori_loop(0, count, body, total, unroll=4)

            def drain(j, carry):
                copy(buf.at[0, 0, 0], targets[0].at[0], osem).wait()
                return carry

            lax.fori_loop(0, total, drain, 0)

        @pl.when(core_ref[0] == 0)
        def _():
            scatter((pk, pv))

        @pl.when(core_ref[0] != 0)
        def _():
            scatter((pv, pk))

    shape = jax.ShapeDtypeStruct((per_source,) + page, direct[0].dtype)
    first = 3 + 2 * shifts
    return pl.pallas_call(
        kernel,
        out_shape=[shape, shape],
        in_specs=[SMEM, SMEM, SMEM] + [ANY] * (2 * shifts + len(pools)),
        out_specs=[ANY, ANY],
        input_output_aliases={first: 0, first + 1: 1} if pools else {},
        scratch_shapes=[
            pltpu.VMEM((2, shifts, count) + page, direct[0].dtype),
            pltpu.SemaphoreType.DMA((2, shifts)),
            pltpu.SemaphoreType.DMA,
        ],
        compiler_params=params(),
        cost_estimate=cost(shifts * count * page[0] * page[1] * 16),
        name="settle_pages",
    )(core, spans, lists, *direct, *swapped, *pools)


def bounds_of(row_of, queries, pages, block):
    n_pages, page_rows, width = pages.shape
    rows = queries.shape[0]
    kv_local = width // HD
    heads = queries.shape[1] // HD
    group = heads // kv_local
    scale = 1.0 / math.sqrt(HD)

    def kernel(row_ref, q_ref, page_ref, out_ref):
        x = page_ref[...]
        low = jnp.min(x, axis=1)
        high = jnp.max(x, axis=1)
        owner = row_ref[...]
        for h in range(kv_local):
            part = slice(h * HD, (h + 1) * HD)
            result = jnp.zeros((group, block), jnp.float32)
            for r in range(rows):
                q = q_ref[r, h * group : (h + 1) * group, :]
                zero = jnp.zeros_like(q)
                dims = (((1,), (1,)), ((), ()))
                both = lax.dot_general(
                    jnp.maximum(q, zero), high[:, part], dims, preferred_element_type=jnp.float32
                ) + lax.dot_general(
                    jnp.minimum(q, zero), low[:, part], dims, preferred_element_type=jnp.float32
                )
                result = jnp.where(owner == r, both, result)
            out_ref[h * group : (h + 1) * group, :] = result * scale

    return pl.pallas_call(
        kernel,
        grid=(n_pages // block,),
        out_shape=jax.ShapeDtypeStruct((heads, n_pages), jnp.float32),
        in_specs=[
            pl.BlockSpec((1, block), lambda i: (0, i)),
            pl.BlockSpec((rows, heads, HD), lambda i: (0, 0, 0)),
            pl.BlockSpec((block, page_rows, width), lambda i: (i, 0, 0)),
        ],
        out_specs=pl.BlockSpec((heads, block), lambda i: (0, i)),
        compiler_params=params(),
        name="bounds",
    )(row_of, queries.reshape(rows, heads, HD), pages)


def attend(page_slots, live, queries, self_keys, self_values, res_k, res_v, pool_k, pool_v):
    rows, k_sel = page_slots.shape
    res_count, page_rows, width = res_k.shape
    kv_local = width // HD
    heads = queries.shape[1] // HD
    group = heads // kv_local
    tokens = k_sel * page_rows
    scale = 1.0 / math.sqrt(HD)

    def kernel(slot_ref, live_ref, q_ref, sk_ref, sv_ref, rk, rv, pk, pv, out_ref, kb, vb, sems):
        for r in range(rows):

            def body(j, carry, r=r):
                slot = slot_ref[r, j]

                @pl.when(slot < res_count)
                def _():
                    copy(rk.at[slot], kb.at[r, j], sems.at[r, 0]).start()
                    copy(rv.at[slot], vb.at[r, j], sems.at[r, 1]).start()

                @pl.when(slot >= res_count)
                def _():
                    copy(pk.at[slot - res_count], kb.at[r, j], sems.at[r, 0]).start()
                    copy(pv.at[slot - res_count], vb.at[r, j], sems.at[r, 1]).start()

                return carry

            lax.fori_loop(0, k_sel, body, 0)
        for r in range(rows):
            copy(kb.at[r], kb.at[r], sems.at[r, 0]).wait()
            copy(vb.at[r], vb.at[r], sems.at[r, 1]).wait()
            alive = live_ref[r : r + 1, :] > 0
            for h in range(kv_local):
                part = slice(h * HD, (h + 1) * HD)
                here = slice(h * group, (h + 1) * group)
                q = q_ref[r, here, :]
                keys = kb[r, :, :, part].reshape(tokens, HD)
                values = vb[r, :, :, part].reshape(tokens, HD)
                scores = (
                    lax.dot_general(
                        q, keys, (((1,), (1,)), ((), ())), preferred_element_type=jnp.float32
                    )
                    * scale
                )
                scores = jnp.where(alive, scores, -1e30)
                self_key = sk_ref[r : r + 1, part].astype(jnp.float32)
                self_score = (
                    jnp.sum(q.astype(jnp.float32) * self_key, axis=1, keepdims=True) * scale
                )
                top = jnp.maximum(jnp.max(scores, axis=1, keepdims=True), self_score)
                weights = jnp.where(alive, jnp.exp(scores - top), 0.0)
                self_weight = jnp.exp(self_score - top)
                total = jnp.sum(weights, axis=1, keepdims=True) + self_weight
                mixed = lax.dot_general(
                    weights.astype(jnp.bfloat16),
                    values,
                    (((1,), (0,)), ((), ())),
                    preferred_element_type=jnp.float32,
                )
                self_rounded = self_weight.astype(jnp.bfloat16).astype(jnp.float32)
                mixed = mixed + self_rounded * sv_ref[r : r + 1, part].astype(jnp.float32)
                out_ref[r, here, :] = (mixed / total).astype(jnp.bfloat16)

    return pl.pallas_call(
        kernel,
        out_shape=jax.ShapeDtypeStruct((rows, heads, HD), jnp.bfloat16),
        in_specs=[SMEM, VMEM, VMEM, VMEM, VMEM, ANY, ANY, ANY, ANY],
        out_specs=VMEM,
        scratch_shapes=[
            pltpu.VMEM((rows, k_sel, page_rows, width), jnp.bfloat16),
            pltpu.VMEM((rows, k_sel, page_rows, width), jnp.bfloat16),
            pltpu.SemaphoreType.DMA((rows, 2)),
        ],
        compiler_params=params(),
        name="attend",
    )(
        page_slots,
        live,
        queries.reshape(rows, heads, HD),
        self_keys,
        self_values,
        res_k,
        res_v,
        pool_k,
        pool_v,
    )


def project(attended, out_weight):
    ranks = lax.axis_size("head")
    here = lax.axis_index("head")
    partial = jnp.dot(attended, out_weight, preferred_element_type=jnp.float32)
    columns = partial.shape[1] // ranks

    def piece(owner):
        return lax.dynamic_slice_in_dim(partial, owner * columns, columns, 1)

    total = piece(here)
    for s in range(1, ranks):
        pairs = [(k, (k + s) % ranks) for k in range(ranks)]
        total = total + lax.ppermute(piece((here + s) % ranks), "head", pairs)
    return total.astype(jnp.bfloat16)


def on_device(
    new_keys,
    new_values,
    page_dest,
    page_slot,
    resident_keys,
    resident_values,
    queries,
    self_keys,
    self_values,
    context_len,
    selected,
    out_weight,
):
    groups = lax.axis_size("grp")
    chips = groups // CORES
    me = lax.axis_index("grp")
    chip, core = me // CORES, me % CORES
    per_source, page_rows = new_keys.shape[:2]
    res_count = resident_keys.shape[0]
    rows_here = queries.shape[0]
    pair_cap = 2 * per_source // groups
    cap = CORES * CORES * pair_cap
    unit = cap // 16
    first, second, ready = 3 * unit, 6 * unit, 5 * unit

    def permute(x, shift):
        return lax.ppermute(x, "grp", [(i, i ^ shift) for i in range(groups)])

    def after(x, *others):
        return lax.optimization_barrier((x, *others))[0]

    core_list = core.reshape(1)
    shifts = jnp.arange(1, chips, dtype=jnp.int32)
    partners = chip ^ shifts
    own_ids = jnp.arange(per_source, dtype=jnp.int32)
    width = cap + 8

    page_counts = (context_len + page_rows - 1) // page_rows
    row_end = jnp.cumsum(page_counts)
    row_start = row_end - page_counts
    slot_ids = jnp.arange(res_count + per_source, dtype=jnp.int32)
    owner_row = jnp.sum((slot_ids[None, :] >= row_end[:, None]).astype(jnp.int32), axis=0)[None]
    page_slots = row_start[:, None] + selected
    within = jnp.arange(page_rows, dtype=jnp.int32)
    live = (
        (selected[:, :, None] * page_rows + within[None, None, :] < context_len[:, None, None])
        .astype(jnp.int32)
        .reshape(rows_here, -1)
    )

    own_info = jnp.stack([page_dest, page_slot])
    infos = jnp.stack([own_info] + [permute(own_info, s * CORES) for s in range(1, chips)])
    infos = jnp.stack([infos, permute(infos, 1)], axis=1)
    dest, slot = infos[:, :, 0], infos[:, :, 1]

    own_sends = invert(
        (page_dest // CORES)[None, :] == partners[:, None],
        jnp.broadcast_to(own_ids, (chips - 1, per_source)),
        first,
    )
    zeros = jnp.zeros((chips - 1,), jnp.int32)
    packed = pack_pages(core_list, zeros, own_sends, first, new_keys, new_values)
    direct0 = [permute(x, (s + 1) * CORES) for s, x in enumerate(packed)]

    ids = jnp.arange(CORES * per_source, dtype=jnp.int32)
    my_dest = after(dest[0].reshape(-1), *packed)
    sends = invert(
        (my_dest // CORES)[None, :] == partners[:, None],
        jnp.broadcast_to(ids, (chips - 1, ids.shape[0])),
        width,
    )
    own_counts = jnp.sum((page_dest // CORES == partners[:, None]).astype(jnp.int32), axis=1)
    send_start = jnp.minimum(own_counts, first)

    new_keys_, new_values_ = lax.optimization_barrier((new_keys, new_values, sends))[:2]
    sib = (permute(new_keys_, 1), permute(new_values_, 1))

    def pack(offset, count, start=send_start):
        return pack_pages(core_list, start + offset, sends, count, new_keys, new_values, sib)

    def send(packed):
        return [permute(x, (s + 1) * CORES) for s, x in enumerate(packed)]

    packed, direct0 = lax.optimization_barrier((pack(0, second), direct0))
    direct1 = send(packed)
    res_bounds = bounds_of(
        owner_row[:, :res_count], queries, after(resident_keys, *packed), res_count
    )

    dest = after(dest, *packed)
    chip_ids = jnp.arange(chips, dtype=jnp.int32)
    counts = jnp.sum((dest[..., None] // CORES == chip_ids).astype(jnp.int32), axis=2)
    early = jnp.minimum(counts, first)
    late = jnp.sum(counts, axis=1, keepdims=True) - early
    late = jnp.where((chip ^ chip_ids)[:, None, None] == chip_ids[None, None, :], 0, late)
    needed = jnp.max(late)

    arrive_dest = jnp.concatenate([dest[1:], dest[1:, ::-1]]).reshape(2 * (chips - 1), -1)
    arrive_slot = jnp.concatenate([slot[1:], slot[1:, ::-1]]).reshape(2 * (chips - 1), -1)
    arrivals = invert(
        arrive_dest // CORES == chip,
        (arrive_dest % CORES) * per_source + arrive_slot,
        width,
    )
    from_early = lax.dynamic_index_in_dim(early, chip, 2, keepdims=False)[1:]
    arrive_start = jnp.concatenate([from_early[:, 0], from_early[:, 1]])

    def spans_at(arrive_start, offset):
        start = arrive_start + offset
        return jnp.stack([start, jnp.full_like(start, width)], axis=1)

    early_spans = jnp.stack([jnp.zeros_like(arrive_start), arrive_start], axis=1)

    locals_ = invert(
        jnp.stack([dest[0, 0] == me, dest[0, 1] == me]),
        own_ids[None, :] * per_source + slot[0],
        pair_cap,
    )

    def settle(spans, direct, pools=()):
        swapped = [permute(x, 1) for x in direct]
        return settle_pages(core_list, spans, arrivals, direct, swapped, per_source, pools)

    pools = settle(early_spans, direct0)
    pools = settle_local(locals_, (new_keys, new_values), sib, pools)

    packed = pack(second, ready)
    packed, direct1, pools, res_bounds, needed, info = lax.optimization_barrier(
        (packed, direct1, pools, res_bounds, needed, (send_start, arrive_start))
    )

    def rest(total):
        def branch(ops):
            packed, direct, pools, (send_start, arrive_start) = ops
            arrived = []
            if total:
                held = min(total, ready)
                arrived.append(send([x[:held] for x in packed]))
            pools = settle(spans_at(arrive_start, 0), direct, pools)
            if total > ready:
                more = pack(second + ready, total - ready, send_start)
                arrived.append(send(more))
            offset = second
            for direct in arrived:
                pools = settle(spans_at(arrive_start, offset), direct, pools)
                offset += ready
            return pools

        return branch

    totals = [k * unit for k in ((0, 1, 2, 3, 4, 5, 7, 10) if chips <= 4 else (10,))]
    which = sum((needed - second > total).astype(jnp.int32) for total in totals[:-1])
    ops = (packed, direct1, pools, info)
    if len(totals) > 1:
        pool_k, pool_v = lax.switch(which, [rest(total) for total in totals], ops)
    else:
        pool_k, pool_v = rest(totals[0])(ops)

    pool_bounds = bounds_of(owner_row[:, res_count:], queries, pool_k, min(128, per_source))
    attended = attend(
        page_slots,
        live,
        queries,
        self_keys,
        self_values,
        resident_keys,
        resident_values,
        pool_k,
        pool_v,
    )
    projected = project(attended.reshape(rows_here, -1), out_weight)
    return pool_k, pool_v, jnp.concatenate([res_bounds, pool_bounds], axis=1), projected


def solution(mesh):
    in_specs = (
        P("grp", None, "head"),
        P("grp", None, "head"),
        P("grp"),
        P("grp"),
        P("grp", None, "head"),
        P("grp", None, "head"),
        P("grp", "head"),
        P("grp", "head"),
        P("grp", "head"),
        P("grp"),
        P("grp", None),
        P("head", None),
    )
    out_specs = (P("grp", None, "head"), P("grp", None, "head"), P("head", "grp"), P("grp", "head"))
    return jax.shard_map(
        on_device, mesh=mesh, in_specs=in_specs, out_specs=out_specs, check_vma=False
    )
```

```python
import functools
import math

import jax
import jax.numpy as jnp
from jax import lax
from jax.experimental import pallas as pl
from jax.experimental.pallas import tpu as pltpu
from jax.sharding import PartitionSpec as P

HD = 128
CORES = 2
ANY = pl.BlockSpec(memory_space=pl.ANY)
SMEM = pl.BlockSpec(memory_space=pltpu.SMEM)
VMEM = pl.BlockSpec(memory_space=pltpu.VMEM)
VMEM_LIMIT = 60 << 20


def params(**kw):
    return pltpu.CompilerParams(vmem_limit_bytes=VMEM_LIMIT, **kw)


def cost(size):
    return pl.CostEstimate(flops=0, bytes_accessed=size // 64, transcendentals=0)


def copy(src, dst, sem):
    return pltpu.make_async_copy(src, dst, sem)


def invert(marks, payloads, width):
    rows, size = marks.shape
    padded = -(-rows // 8) * 8
    marks = jnp.pad(marks.astype(jnp.int32), ((0, padded - rows), (0, 0)))
    payloads = jnp.pad(payloads, ((0, padded - rows), (0, 0)))

    def kernel(mark_ref, payload_ref, out_ref):
        marked = mark_ref[...]
        upto = (
            lax.broadcasted_iota(jnp.int32, (size, size), 0)
            <= lax.broadcasted_iota(jnp.int32, (size, size), 1)
        ).astype(jnp.float32)
        ranks = jnp.dot(
            marked.astype(jnp.float32).astype(jnp.bfloat16),
            upto.astype(jnp.bfloat16),
            preferred_element_type=jnp.float32,
        )
        ranks = jnp.where(marked > 0, ranks - 1.0, -1.0).astype(jnp.int32)
        places = lax.broadcasted_iota(jnp.int32, (width, size), 0)
        parts = lax.broadcasted_iota(jnp.int32, (8, size), 0)
        for t in range(rows):
            hits = (ranks[t : t + 1, :] == places).astype(jnp.float32).astype(jnp.bfloat16)
            value = payload_ref[t : t + 1, :]
            pieces = jnp.where(parts < 3, (value >> (7 * jnp.minimum(parts, 2))) & 127, 1)
            found = lax.dot_general(
                pieces.astype(jnp.float32).astype(jnp.bfloat16),
                hits,
                (((1,), (1,)), ((), ())),
                preferred_element_type=jnp.float32,
            ).astype(jnp.int32)
            whole = found[0:1] + found[1:2] * 128 + found[2:3] * 16384
            out_ref[t : t + 1, :] = jnp.where(found[3:4] > 0, whole, -1)

    return pl.pallas_call(
        kernel,
        out_shape=jax.ShapeDtypeStruct((rows, width), jnp.int32),
        in_specs=[VMEM, VMEM],
        out_specs=VMEM,
        compiler_params=params(),
        name="invert",
    )(marks, payloads)


def triangle(size):
    row = lax.broadcasted_iota(jnp.int32, (size, size), 0)
    column = lax.broadcasted_iota(jnp.int32, (size, size), 1)
    return (row <= column).astype(jnp.float32).astype(jnp.bfloat16)


def running(marks, upto):
    return jnp.dot(marks.astype(jnp.bfloat16), upto, preferred_element_type=jnp.float32)


def place(rank_row, payload_row, width):
    size = rank_row.shape[1]
    places = lax.broadcasted_iota(jnp.int32, (width, size), 0)
    hits = (rank_row.astype(jnp.int32) == places).astype(jnp.float32).astype(jnp.bfloat16)
    parts = lax.broadcasted_iota(jnp.int32, (8, size), 0)
    pieces = jnp.where(parts < 2, (payload_row >> (7 * jnp.minimum(parts, 1))) & 127, 1)
    found = lax.dot_general(
        pieces.astype(jnp.float32).astype(jnp.bfloat16),
        hits,
        (((1,), (1,)), ((), ())),
        preferred_element_type=jnp.float32,
    ).astype(jnp.int32)
    return jnp.where(found[2:3] > 0, found[0:1] + found[1:2] * 128, -1)


def first_lists(me, dest, shifts, width):
    size = dest.shape[1]
    padded = -(-shifts // 8) * 8

    def kernel(me_ref, dest_ref, out_ref):
        away = (dest_ref[...] ^ me_ref[0]) // CORES
        shift = lax.broadcasted_iota(jnp.int32, (padded, size), 0) + 1
        marks = (away == shift).astype(jnp.float32)
        ranks = jnp.where(marks > 0, running(marks, triangle(size)) - 1.0, -1.0)
        ids = lax.broadcasted_iota(jnp.int32, (1, size), 1)
        for t in range(shifts):
            out_ref[t : t + 1, :] = place(ranks[t : t + 1, :], ids, width)

    return pl.pallas_call(
        kernel,
        out_shape=jax.ShapeDtypeStruct((shifts, width), jnp.int32),
        in_specs=[SMEM, VMEM],
        out_specs=VMEM,
        compiler_params=params(),
        name="first_lists",
    )(me, dest)


def wanted_of(owner, slot, flags):
    rows, size = slot.shape
    owners, slots = flags.shape

    def kernel(owner_ref, slot_ref, flag_ref, out_ref):
        flag = flag_ref[...].astype(jnp.float32).astype(jnp.bfloat16)
        for r in range(rows):
            spot = lax.broadcasted_iota(jnp.int32, (slots, size), 0)
            hits = (slot_ref[r : r + 1, :] == spot).astype(jnp.float32).astype(jnp.bfloat16)
            found = jnp.dot(flag, hits, preferred_element_type=jnp.float32)
            who = lax.broadcasted_iota(jnp.int32, (owners, size), 0)
            out_ref[r : r + 1, :] = jnp.sum(
                jnp.where(owner_ref[r : r + 1, :] == who, found, 0.0), axis=0, keepdims=True
            )

    return pl.pallas_call(
        kernel,
        out_shape=jax.ShapeDtypeStruct((rows, size), jnp.float32),
        in_specs=[VMEM, VMEM, VMEM],
        out_specs=VMEM,
        compiler_params=params(),
        name="wanted_of",
    )(owner, slot, flags)


def full_lists(marks, wanted, payloads, rows, own, first, width):
    padded, size = marks.shape

    def kernel(mark_ref, want_ref, payload_ref, out_ref, start_ref):
        upto = triangle(size)
        marks = mark_ref[...].astype(jnp.float32)
        want = want_ref[...]
        count = running(marks, upto)
        column = lax.broadcasted_iota(jnp.int32, (padded, size), 1)
        early = jnp.where((column < own) & (count <= first), marks, 0.0)
        wanted = (marks - early) * want
        others = (marks - early) * (1.0 - want)
        n_early = jnp.sum(early, axis=1, keepdims=True)
        n_wanted = jnp.sum(wanted, axis=1, keepdims=True)
        ranks = jnp.where(
            early > 0,
            count - 1.0,
            jnp.where(
                wanted > 0,
                n_early + running(wanted, upto) - 1.0,
                jnp.where(others > 0, n_early + n_wanted + running(others, upto) - 1.0, -1.0),
            ),
        )
        start_ref[...] = jnp.broadcast_to(n_early, start_ref.shape).astype(jnp.int32)
        for t in range(rows):
            out_ref[t : t + 1, :] = place(
                ranks[t : t + 1, :], payload_ref[t : t + 1, :], width
            )

    lists, starts = pl.pallas_call(
        kernel,
        out_shape=[
            jax.ShapeDtypeStruct((rows, width), jnp.int32),
            jax.ShapeDtypeStruct((padded, 128), jnp.int32),
        ],
        in_specs=[VMEM, VMEM, VMEM],
        out_specs=[VMEM, VMEM],
        compiler_params=params(),
        name="full_lists",
    )(marks, wanted, payloads)
    return lists, starts[:rows, 0]


def padded_rows(x, rows):
    return jnp.pad(x, ((0, rows - x.shape[0]), (0, 0)))


def pack_pages(core, starts, lists, pieces, own_k, own_v, sib=None):
    count = sum(pieces)
    shifts, width = lists.shape
    per_source = own_k.shape[0]
    page = own_k.shape[1:]
    sibs = () if sib is None else sib

    def kernel(core_ref, start_ref, list_ref, ok, ov, *rest):
        sib_refs, rest = rest[: len(sibs)], rest[len(sibs) :]
        outs, (buf, sems, out_sems) = rest[:-3], rest[-3:]

        def outgoing(s):
            low = 0
            for p, piece in enumerate(pieces):
                yield copy(
                    buf.at[s, pl.ds(low, piece)], outs[p * shifts + s], out_sems.at[p * shifts + s]
                )
                low += piece

        def gather(own, other):
            for s in range(shifts):
                start = start_ref[s]

                def body(j, carry, s=s, start=start):
                    i = jnp.maximum(list_ref[s, jnp.minimum(start + j, width - 1)], 0)
                    if other is None:
                        copy(own.at[jnp.minimum(i, per_source - 1)], buf.at[s, j], sems.at[s]).start()
                    else:

                        @pl.when(i < per_source)
                        def _():
                            copy(own.at[i], buf.at[s, j], sems.at[s]).start()

                        @pl.when(i >= per_source)
                        def _():
                            copy(other.at[i - per_source], buf.at[s, j], sems.at[s]).start()

                    return carry

                lax.fori_loop(0, count, body, 0, unroll=4)

        @pl.when(core_ref[0] == 0)
        def _():
            gather(ok, sib_refs[0] if sibs else None)

        @pl.when(core_ref[0] != 0)
        def _():
            gather(ov, sib_refs[1] if sibs else None)

        for s in range(shifts):
            copy(buf.at[s], buf.at[s], sems.at[s]).wait()
            for sent in outgoing(s):
                sent.start()
        for s in range(shifts):
            for sent in outgoing(s):
                sent.wait()

    packed = pl.pallas_call(
        kernel,
        out_shape=[
            jax.ShapeDtypeStruct((piece,) + page, own_k.dtype)
            for piece in pieces
            for _ in range(shifts)
        ],
        in_specs=[SMEM, SMEM, SMEM, ANY, ANY] + [ANY] * len(sibs),
        out_specs=[ANY] * (shifts * len(pieces)),
        scratch_shapes=[
            pltpu.VMEM((shifts, count) + page, own_k.dtype),
            pltpu.SemaphoreType.DMA((shifts,)),
            pltpu.SemaphoreType.DMA((shifts * len(pieces),)),
        ],
        compiler_params=params(),
        cost_estimate=cost(shifts * count * page[0] * page[1] * 8),
        name="pack_pages",
    )(core, starts, lists, own_k, own_v, *sibs)
    return [packed[p * shifts : (p + 1) * shifts] for p in range(len(pieces))]


def settle_local(lists, own, sib, pools):
    count = lists.shape[1]
    per_source = own[0].shape[0]
    page = own[0].shape[1:]

    def kernel(list_ref, *rest):
        sources = (rest[0:2], rest[2:4])
        pk, pv, buf, sem, osem = rest[6:]
        targets = (pk, pv)

        def each(f):
            total = 0
            for who in range(2):

                def body(j, n, who=who):
                    v = list_ref[who, j]

                    @pl.when(v >= 0)
                    def _():
                        f(who, j, v // per_source, v % per_source)

                    return n + jnp.where(v >= 0, 2, 0)

                total = lax.fori_loop(0, count, body, total, unroll=2)
            return total

        def gather(who, j, row, slot):
            for kind in range(2):
                copy(sources[who][kind].at[row], buf.at[kind, who, j], sem).start()

        def scatter(who, j, row, slot):
            for kind in range(2):
                copy(buf.at[kind, who, j], targets[kind].at[slot], osem).start()

        def drain(a_sem):
            def body(j, carry):
                copy(buf.at[0, 0, 0], pk.at[0], a_sem).wait()
                return carry

            return body

        lax.fori_loop(0, each(gather), drain(sem), 0)
        lax.fori_loop(0, each(scatter), drain(osem), 0)

    shape = jax.ShapeDtypeStruct(own[0].shape, own[0].dtype)
    return pl.pallas_call(
        kernel,
        out_shape=[shape, shape],
        in_specs=[SMEM] + [ANY] * 6,
        out_specs=[ANY, ANY],
        input_output_aliases={5: 0, 6: 1},
        scratch_shapes=[
            pltpu.VMEM((2, 2, count) + page, own[0].dtype),
            pltpu.SemaphoreType.DMA,
            pltpu.SemaphoreType.DMA,
        ],
        compiler_params=params(),
        cost_estimate=cost(count * page[0] * page[1] * 32),
        name="settle_local",
    )(lists, *own, *sib, *pools)


def settle_pages(core, spans, lists, direct, swapped, per_source, pools=()):
    shifts = len(direct[0])
    pieces = [piece[0].shape[0] for piece in direct]
    n_arrays = shifts * len(pieces)
    page = direct[0][0].shape[1:]
    width = lists.shape[1]

    def kernel(core_ref, span_ref, list_ref, *rest):
        arrived = (rest[:n_arrays], rest[n_arrays : 2 * n_arrays])
        pk, pv, buf, sems, osem = rest[2 * n_arrays + len(pools) :]
        low = core_ref[0] * per_source

        def incoming(k, p, s):
            where = pl.ds(sum(pieces[:p]), pieces[p])
            i = p * shifts + s
            return copy(arrived[k][i], buf.at[k, s, where], sems.at[k, i])

        order = [
            (k, p, s) for s in range(shifts) for k in range(2) for p in range(len(pieces))
        ]
        for k, p, s in order:
            incoming(k, p, s).start()

        def scatter(targets):
            total = 0
            for k, p, s in order:
                incoming(k, p, s).wait()
                if p + 1 < len(pieces):
                    continue
                row = k * shifts + s
                start, limit = span_ref[row, 0], span_ref[row, 1]

                def body(j, n, s=s, k=k, row=row, start=start, limit=limit):
                    place = start + j
                    slot = list_ref[row, jnp.minimum(place, width - 1)] - low
                    mine = (slot >= 0) & (slot < per_source) & (place < limit)

                    @pl.when(mine)
                    def _():
                        copy(buf.at[k, s, j], targets[k].at[slot], osem).start()

                    return n + jnp.where(mine, 1, 0)

                total = lax.fori_loop(0, sum(pieces), body, total, unroll=4)

            def drain(j, carry):
                copy(buf.at[0, 0, 0], targets[0].at[0], osem).wait()
                return carry

            lax.fori_loop(0, total, drain, 0)

        @pl.when(core_ref[0] == 0)
        def _():
            scatter((pk, pv))

        @pl.when(core_ref[0] != 0)
        def _():
            scatter((pv, pk))

    dtype = direct[0][0].dtype
    shape = jax.ShapeDtypeStruct((per_source,) + page, dtype)
    first = 3 + 2 * n_arrays
    return pl.pallas_call(
        kernel,
        out_shape=[shape, shape],
        in_specs=[SMEM, SMEM, SMEM] + [ANY] * (2 * n_arrays + len(pools)),
        out_specs=[ANY, ANY],
        input_output_aliases={first: 0, first + 1: 1} if pools else {},
        scratch_shapes=[
            pltpu.VMEM((2, shifts, sum(pieces)) + page, dtype),
            pltpu.SemaphoreType.DMA((2, n_arrays)),
            pltpu.SemaphoreType.DMA,
        ],
        compiler_params=params(),
        cost_estimate=cost(shifts * sum(pieces) * page[0] * page[1] * 16),
        name="settle_pages",
    )(core, spans, lists, *sum(direct, []), *sum(swapped, []), *pools)


def bounds_of(row_of, queries, pages, block):
    n_pages, page_rows, width = pages.shape
    rows = queries.shape[0]
    kv_local = width // HD
    heads = queries.shape[1] // HD
    group = heads // kv_local
    scale = 1.0 / math.sqrt(HD)

    def kernel(row_ref, q_ref, page_ref, out_ref):
        x = page_ref[...]
        low = jnp.min(x, axis=1)
        high = jnp.max(x, axis=1)
        owner = row_ref[...]
        for h in range(kv_local):
            part = slice(h * HD, (h + 1) * HD)
            result = jnp.zeros((group, block), jnp.float32)
            for r in range(rows):
                q = q_ref[r, h * group : (h + 1) * group, :]
                zero = jnp.zeros_like(q)
                dims = (((1,), (1,)), ((), ()))
                both = lax.dot_general(
                    jnp.maximum(q, zero), high[:, part], dims, preferred_element_type=jnp.float32
                ) + lax.dot_general(
                    jnp.minimum(q, zero), low[:, part], dims, preferred_element_type=jnp.float32
                )
                result = jnp.where(owner == r, both, result)
            out_ref[h * group : (h + 1) * group, :] = result * scale

    return pl.pallas_call(
        kernel,
        grid=(n_pages // block,),
        out_shape=jax.ShapeDtypeStruct((heads, n_pages), jnp.float32),
        in_specs=[
            pl.BlockSpec((1, block), lambda i: (0, i)),
            pl.BlockSpec((rows, heads, HD), lambda i: (0, 0, 0)),
            pl.BlockSpec((block, page_rows, width), lambda i: (i, 0, 0)),
        ],
        out_specs=pl.BlockSpec((heads, block), lambda i: (0, i)),
        compiler_params=params(),
        name="bounds",
    )(row_of, queries.reshape(rows, heads, HD), pages)


def attend(page_slots, live, queries, self_keys, self_values, res_k, res_v, pool_k, pool_v):
    rows, k_sel = page_slots.shape
    res_count, page_rows, width = res_k.shape
    kv_local = width // HD
    heads = queries.shape[1] // HD
    group = heads // kv_local
    tokens = k_sel * page_rows
    scale = 1.0 / math.sqrt(HD)

    def kernel(slot_ref, live_ref, q_ref, sk_ref, sv_ref, rk, rv, pk, pv, out_ref, kb, vb, sems):
        for r in range(rows):

            def body(j, carry, r=r):
                slot = slot_ref[r, j]

                @pl.when(slot < res_count)
                def _():
                    copy(rk.at[slot], kb.at[r, j], sems.at[r, 0]).start()
                    copy(rv.at[slot], vb.at[r, j], sems.at[r, 1]).start()

                @pl.when(slot >= res_count)
                def _():
                    copy(pk.at[slot - res_count], kb.at[r, j], sems.at[r, 0]).start()
                    copy(pv.at[slot - res_count], vb.at[r, j], sems.at[r, 1]).start()

                return carry

            lax.fori_loop(0, k_sel, body, 0)
        for r in range(rows):
            copy(kb.at[r], kb.at[r], sems.at[r, 0]).wait()
            copy(vb.at[r], vb.at[r], sems.at[r, 1]).wait()
            alive = live_ref[r : r + 1, :] > 0
            for h in range(kv_local):
                part = slice(h * HD, (h + 1) * HD)
                here = slice(h * group, (h + 1) * group)
                q = q_ref[r, here, :]
                keys = kb[r, :, :, part].reshape(tokens, HD)
                values = vb[r, :, :, part].reshape(tokens, HD)
                scores = (
                    lax.dot_general(
                        q, keys, (((1,), (1,)), ((), ())), preferred_element_type=jnp.float32
                    )
                    * scale
                )
                scores = jnp.where(alive, scores, -1e30)
                self_key = sk_ref[r : r + 1, part].astype(jnp.float32)
                self_score = (
                    jnp.sum(q.astype(jnp.float32) * self_key, axis=1, keepdims=True) * scale
                )
                top = jnp.maximum(jnp.max(scores, axis=1, keepdims=True), self_score)
                weights = jnp.where(alive, jnp.exp(scores - top), 0.0)
                self_weight = jnp.exp(self_score - top)
                total = jnp.sum(weights, axis=1, keepdims=True) + self_weight
                mixed = lax.dot_general(
                    weights.astype(jnp.bfloat16),
                    values,
                    (((1,), (0,)), ((), ())),
                    preferred_element_type=jnp.float32,
                )
                self_rounded = self_weight.astype(jnp.bfloat16).astype(jnp.float32)
                mixed = mixed + self_rounded * sv_ref[r : r + 1, part].astype(jnp.float32)
                out_ref[r, here, :] = (mixed / total).astype(jnp.bfloat16)

    return pl.pallas_call(
        kernel,
        out_shape=jax.ShapeDtypeStruct((rows, heads, HD), jnp.bfloat16),
        in_specs=[SMEM, VMEM, VMEM, VMEM, VMEM, ANY, ANY, ANY, ANY],
        out_specs=VMEM,
        scratch_shapes=[
            pltpu.VMEM((rows, k_sel, page_rows, width), jnp.bfloat16),
            pltpu.VMEM((rows, k_sel, page_rows, width), jnp.bfloat16),
            pltpu.SemaphoreType.DMA((rows, 2)),
        ],
        compiler_params=params(),
        name="attend",
    )(
        page_slots,
        live,
        queries.reshape(rows, heads, HD),
        self_keys,
        self_values,
        res_k,
        res_v,
        pool_k,
        pool_v,
    )


def project(partial):
    ranks = lax.axis_size("head")
    here = lax.axis_index("head")
    columns = partial.shape[1] // ranks

    def piece(owner):
        return lax.dynamic_slice_in_dim(partial, owner * columns, columns, 1)

    total = piece(here)
    for s in range(1, ranks):
        pairs = [(k, (k + s) % ranks) for k in range(ranks)]
        total = total + lax.ppermute(piece((here + s) % ranks), "head", pairs)
    return total.astype(jnp.bfloat16)


def on_device(
    new_keys,
    new_values,
    page_dest,
    page_slot,
    resident_keys,
    resident_values,
    queries,
    self_keys,
    self_values,
    context_len,
    selected,
    out_weight,
):
    groups = lax.axis_size("grp")
    chips = groups // CORES
    me = lax.axis_index("grp")
    chip, core = me // CORES, me % CORES
    per_source, page_rows = new_keys.shape[:2]
    res_count = resident_keys.shape[0]
    rows_here = queries.shape[0]
    pair_cap = 2 * per_source // groups
    cap = CORES * CORES * pair_cap
    unit = cap // 16
    first, second, third = 3 * unit, 4 * unit, 3 * unit
    shifts = chips - 1

    def permute(x, shift):
        return lax.ppermute(x, "grp", [(i, i ^ shift) for i in range(groups)])

    def after(x, *others):
        return lax.optimization_barrier((x, *others))[0]

    def send(packed):
        return [[permute(x, (s + 1) * CORES) for s, x in enumerate(piece)] for piece in packed]

    me_list, core_list = me.reshape(1), core.reshape(1)
    own_ids = jnp.arange(per_source, dtype=jnp.int32)
    width = cap + 8

    page_counts = (context_len + page_rows - 1) // page_rows
    row_end = jnp.cumsum(page_counts)
    row_start = row_end - page_counts
    page_slots = row_start[:, None] + selected
    chosen = (page_slots.reshape(-1, 1) - res_count == own_ids[None, :]).astype(jnp.int32)
    chosen = jnp.max(chosen, axis=0)

    own_info = jnp.stack([page_dest, page_slot, chosen])
    infos = jnp.stack([own_info] + [permute(own_info, s * CORES) for s in range(1, chips)])
    infos = jnp.stack([infos, permute(infos, 1)], axis=1)
    dest, slot, flags = infos[:, :, 0], infos[:, :, 1], infos[:, :, 2]
    flags = flags.reshape(groups, per_source)

    own_sends = first_lists(me_list, page_dest[None], shifts, first)
    packed = pack_pages(
        core_list, jnp.zeros((shifts,), jnp.int32), own_sends, [first], new_keys, new_values
    )
    direct0 = send(packed)

    dest, slot = lax.optimization_barrier((dest, slot, packed))[:2]
    away = dest ^ me
    padded = -(-shifts // 8) * 8
    shift_ids = jnp.arange(1, padded + 1, dtype=jnp.int32)
    chip_away = (away[0] // CORES).reshape(1, -1)
    wanted = wanted_of(away[0], slot[0], flags).reshape(1, -1)
    ids = jnp.arange(CORES * per_source, dtype=jnp.int32)[None]
    sends, send_start = full_lists(
        (chip_away == shift_ids[:, None]).astype(jnp.int32),
        jnp.broadcast_to(wanted, (padded, wanted.shape[1])),
        jnp.broadcast_to(ids, (padded, ids.shape[1])),
        shifts,
        per_source,
        first,
        width,
    )

    new_keys_, new_values_ = lax.optimization_barrier((new_keys, new_values, packed))[:2]
    sib = (permute(new_keys_, 1), permute(new_values_, 1))

    def pack(offset, pieces, start=send_start):
        return pack_pages(core_list, start + offset, sends, pieces, new_keys, new_values, sib)

    packed = pack(0, [second])
    dest, slot = lax.optimization_barrier((dest, slot, packed))[:2]

    chip_ids = jnp.arange(chips, dtype=jnp.int32)
    counts = jnp.sum((dest[..., None] // CORES == chip_ids).astype(jnp.int32), axis=2)
    late = jnp.sum(counts, axis=1, keepdims=True) - jnp.minimum(counts, first)
    late = jnp.where((chip ^ chip_ids)[:, None, None] == chip_ids[None, None, :], 0, late)
    needed = jnp.max(late)

    def both_kinds(x):
        x = jnp.concatenate([x[1:], x[1:, ::-1]]).reshape(2 * shifts, -1)
        return padded_rows(x, -(-2 * shifts // 8) * 8)

    arrive_wanted = wanted_of(
        (dest ^ me)[1:].reshape(shifts * CORES, -1), slot[1:].reshape(shifts * CORES, -1), flags
    ).reshape(shifts, CORES, -1)
    arrive_wanted = jnp.concatenate([wanted.reshape(1, CORES, -1), arrive_wanted])
    to_chip = (dest[..., None] // CORES == chip_ids).astype(jnp.float32)
    most_wanted = jnp.max(jnp.sum(arrive_wanted[..., None] * to_chip, axis=(1, 2)))
    soon = most_wanted <= second
    arrivals, arrive_start = full_lists(
        both_kinds((dest // CORES == chip).astype(jnp.int32)),
        both_kinds(arrive_wanted),
        both_kinds((dest % CORES) * per_source + slot),
        2 * shifts,
        per_source,
        first,
        width,
    )

    packed, direct0, dest, slot, arrivals, arrive_start = lax.optimization_barrier(
        (packed, direct0, dest, slot, arrivals, arrive_start)
    )
    direct1 = send(packed)

    def spans_at(arrive_start, offset):
        start = arrive_start + offset
        return jnp.stack([start, jnp.full_like(start, width)], axis=1)

    early_spans = jnp.stack([jnp.zeros_like(arrive_start), arrive_start], axis=1)

    locals_ = invert(
        jnp.stack([dest[0, 0] == me, dest[0, 1] == me]),
        own_ids[None, :] * per_source + slot[0],
        pair_cap,
    )

    def settle(spans, direct, pools=()):
        swapped = [[permute(x, 1) for x in piece] for piece in direct]
        return settle_pages(core_list, spans, arrivals, direct, swapped, per_source, pools)

    slot_ids = jnp.arange(res_count + per_source, dtype=jnp.int32)
    owner_row = jnp.sum((slot_ids[None, :] >= row_end[:, None]).astype(jnp.int32), axis=0)[None]
    res_bounds = bounds_of(
        owner_row[:, :res_count], queries, after(resident_keys, packed), res_count
    )
    pools = settle(early_spans, direct0)
    pools = settle_local(locals_, (new_keys, new_values), sib, pools)

    held = [unit // 2, unit // 2, unit // 2]
    more = [unit // 2, unit, unit, 2 * unit, 3 * unit + unit // 2]
    packed, kept, direct1, pools, res_bounds = lax.optimization_barrier(
        (
            pack(second, [third]),
            pack(second + third, held),
            direct1,
            pools,
            res_bounds,
        )
    )
    direct2 = send(packed)
    pools = settle(spans_at(arrive_start, 0), direct1, pools)

    within = jnp.arange(page_rows, dtype=jnp.int32)
    live = (
        (selected[:, :, None] * page_rows + within[None, None, :] < context_len[:, None, None])
        .astype(jnp.int32)
        .reshape(rows_here, -1)
    )

    def decode(pools):
        attended = attend(
            page_slots,
            live,
            queries,
            self_keys,
            self_values,
            resident_keys,
            resident_values,
            *pools,
        )
        return project(
            jnp.dot(attended.reshape(rows_here, -1), out_weight, preferred_element_type=jnp.float32)
        )

    projected = decode(pools)

    kept, direct2, pools, needed, soon, projected, info = lax.optimization_barrier(
        (
            kept,
            direct2,
            pools,
            needed,
            soon,
            projected,
            (send_start, arrive_start),
        )
    )

    def rest(n_pieces):
        def branch(ops):
            packed, direct, pools, (send_start, arrive_start) = ops
            arrived = send(packed[:n_pieces])
            pools = settle(spans_at(arrive_start, second), direct, pools)
            pools, arrived = lax.optimization_barrier((pools, arrived))
            if n_pieces > len(held):
                late = pack(second + third + sum(held), more[: n_pieces - len(held)], send_start)
                arrived = arrived + send(late)
            if arrived:
                pools = settle(spans_at(arrive_start, second + third), arrived, pools)
            return pools

        return branch

    sizes = held + more
    totals = [sum(sizes[:n]) for n in range(len(sizes) + 1)]
    left = needed - second - third
    which = sum((left > total).astype(jnp.int32) for total in totals[:-1])
    ops = (kept, direct2, pools, info)
    if chips <= 4:
        pools = lax.switch(which, [rest(n) for n in range(len(sizes) + 1)], ops)
    else:
        pools = rest(len(sizes))(ops)
    pool_k, pool_v = pools
    projected = lax.cond(soon, lambda pools: projected, decode, pools)

    pool_bounds = bounds_of(owner_row[:, res_count:], queries, pool_k, min(128, per_source))
    return pool_k, pool_v, jnp.concatenate([res_bounds, pool_bounds], axis=1), projected


def solution(mesh):
    in_specs = (
        P("grp", None, "head"),
        P("grp", None, "head"),
        P("grp"),
        P("grp"),
        P("grp", None, "head"),
        P("grp", None, "head"),
        P("grp", "head"),
        P("grp", "head"),
        P("grp", "head"),
        P("grp"),
        P("grp", None),
        P("head", None),
    )
    out_specs = (P("grp", None, "head"), P("grp", None, "head"), P("head", "grp"), P("grp", "head"))
    return jax.shard_map(
        on_device, mesh=mesh, in_specs=in_specs, out_specs=out_specs, check_vma=False
    )
```

```python
import functools
import math

import jax
import jax.numpy as jnp
from jax import lax
from jax.experimental import pallas as pl
from jax.experimental.pallas import tpu as pltpu
from jax.sharding import PartitionSpec as P

HD = 128
CORES = 2
ANY = pl.BlockSpec(memory_space=pl.ANY)
SMEM = pl.BlockSpec(memory_space=pltpu.SMEM)
VMEM = pl.BlockSpec(memory_space=pltpu.VMEM)
VMEM_LIMIT = 60 << 20


def params(**kw):
    return pltpu.CompilerParams(vmem_limit_bytes=VMEM_LIMIT, **kw)


def cost(size):
    return pl.CostEstimate(flops=0, bytes_accessed=size // 64, transcendentals=0)


def copy(src, dst, sem):
    return pltpu.make_async_copy(src, dst, sem)


def invert(marks, payloads, width):
    rows, size = marks.shape
    padded = -(-rows // 8) * 8
    marks = jnp.pad(marks.astype(jnp.int32), ((0, padded - rows), (0, 0)))
    payloads = jnp.pad(payloads, ((0, padded - rows), (0, 0)))

    def kernel(mark_ref, payload_ref, out_ref):
        marked = mark_ref[...]
        upto = (
            lax.broadcasted_iota(jnp.int32, (size, size), 0)
            <= lax.broadcasted_iota(jnp.int32, (size, size), 1)
        ).astype(jnp.float32)
        ranks = jnp.dot(
            marked.astype(jnp.float32).astype(jnp.bfloat16),
            upto.astype(jnp.bfloat16),
            preferred_element_type=jnp.float32,
        )
        ranks = jnp.where(marked > 0, ranks - 1.0, -1.0).astype(jnp.int32)
        places = lax.broadcasted_iota(jnp.int32, (width, size), 0)
        parts = lax.broadcasted_iota(jnp.int32, (8, size), 0)
        for t in range(rows):
            hits = (ranks[t : t + 1, :] == places).astype(jnp.float32).astype(jnp.bfloat16)
            value = payload_ref[t : t + 1, :]
            pieces = jnp.where(parts < 3, (value >> (7 * jnp.minimum(parts, 2))) & 127, 1)
            found = lax.dot_general(
                pieces.astype(jnp.float32).astype(jnp.bfloat16),
                hits,
                (((1,), (1,)), ((), ())),
                preferred_element_type=jnp.float32,
            ).astype(jnp.int32)
            whole = found[0:1] + found[1:2] * 128 + found[2:3] * 16384
            out_ref[t : t + 1, :] = jnp.where(found[3:4] > 0, whole, -1)

    return pl.pallas_call(
        kernel,
        out_shape=jax.ShapeDtypeStruct((rows, width), jnp.int32),
        in_specs=[VMEM, VMEM],
        out_specs=VMEM,
        compiler_params=params(),
        name="invert",
    )(marks, payloads)


def triangle(size):
    row = lax.broadcasted_iota(jnp.int32, (size, size), 0)
    column = lax.broadcasted_iota(jnp.int32, (size, size), 1)
    return (row <= column).astype(jnp.float32).astype(jnp.bfloat16)


def running(marks, upto):
    return jnp.dot(marks.astype(jnp.bfloat16), upto, preferred_element_type=jnp.float32)


def place(rank_row, payload_row, width):
    size = rank_row.shape[1]
    places = lax.broadcasted_iota(jnp.int32, (width, size), 0)
    hits = (rank_row.astype(jnp.int32) == places).astype(jnp.float32).astype(jnp.bfloat16)
    parts = lax.broadcasted_iota(jnp.int32, (8, size), 0)
    pieces = jnp.where(parts < 2, (payload_row >> (7 * jnp.minimum(parts, 1))) & 127, 1)
    found = lax.dot_general(
        pieces.astype(jnp.float32).astype(jnp.bfloat16),
        hits,
        (((1,), (1,)), ((), ())),
        preferred_element_type=jnp.float32,
    ).astype(jnp.int32)
    return jnp.where(found[2:3] > 0, found[0:1] + found[1:2] * 128, -1)


def first_lists(me, dest, shifts, width):
    size = dest.shape[1]
    padded = -(-shifts // 8) * 8

    def kernel(me_ref, dest_ref, out_ref):
        away = (dest_ref[...] ^ me_ref[0]) // CORES
        shift = lax.broadcasted_iota(jnp.int32, (padded, size), 0) + 1
        marks = (away == shift).astype(jnp.float32)
        ranks = jnp.where(marks > 0, running(marks, triangle(size)) - 1.0, -1.0)
        ids = lax.broadcasted_iota(jnp.int32, (1, size), 1)
        for t in range(shifts):
            out_ref[t : t + 1, :] = place(ranks[t : t + 1, :], ids, width)

    return pl.pallas_call(
        kernel,
        out_shape=jax.ShapeDtypeStruct((shifts, width), jnp.int32),
        in_specs=[SMEM, VMEM],
        out_specs=VMEM,
        compiler_params=params(),
        name="first_lists",
    )(me, dest)


def wanted_of(owner, slot, flags):
    rows, size = slot.shape
    owners, slots = flags.shape

    def kernel(owner_ref, slot_ref, flag_ref, out_ref):
        flag = flag_ref[...].astype(jnp.float32).astype(jnp.bfloat16)
        for r in range(rows):
            spot = lax.broadcasted_iota(jnp.int32, (slots, size), 0)
            hits = (slot_ref[r : r + 1, :] == spot).astype(jnp.float32).astype(jnp.bfloat16)
            found = jnp.dot(flag, hits, preferred_element_type=jnp.float32)
            who = lax.broadcasted_iota(jnp.int32, (owners, size), 0)
            out_ref[r : r + 1, :] = jnp.sum(
                jnp.where(owner_ref[r : r + 1, :] == who, found, 0.0), axis=0, keepdims=True
            )

    return pl.pallas_call(
        kernel,
        out_shape=jax.ShapeDtypeStruct((rows, size), jnp.float32),
        in_specs=[VMEM, VMEM, VMEM],
        out_specs=VMEM,
        compiler_params=params(),
        name="wanted_of",
    )(owner, slot, flags)


def full_lists(marks, wanted, payloads, rows, own, first, width):
    padded, size = marks.shape

    def kernel(mark_ref, want_ref, payload_ref, out_ref, start_ref):
        upto = triangle(size)
        marks = mark_ref[...].astype(jnp.float32)
        want = want_ref[...]
        count = running(marks, upto)
        column = lax.broadcasted_iota(jnp.int32, (padded, size), 1)
        early = jnp.where((column < own) & (count <= first), marks, 0.0)
        wanted = (marks - early) * want
        others = (marks - early) * (1.0 - want)
        n_early = jnp.sum(early, axis=1, keepdims=True)
        n_wanted = jnp.sum(wanted, axis=1, keepdims=True)
        ranks = jnp.where(
            early > 0,
            count - 1.0,
            jnp.where(
                wanted > 0,
                n_early + running(wanted, upto) - 1.0,
                jnp.where(others > 0, n_early + n_wanted + running(others, upto) - 1.0, -1.0),
            ),
        )
        start_ref[...] = jnp.broadcast_to(n_early, start_ref.shape).astype(jnp.int32)
        for t in range(rows):
            out_ref[t : t + 1, :] = place(
                ranks[t : t + 1, :], payload_ref[t : t + 1, :], width
            )

    lists, starts = pl.pallas_call(
        kernel,
        out_shape=[
            jax.ShapeDtypeStruct((rows, width), jnp.int32),
            jax.ShapeDtypeStruct((padded, 128), jnp.int32),
        ],
        in_specs=[VMEM, VMEM, VMEM],
        out_specs=[VMEM, VMEM],
        compiler_params=params(),
        name="full_lists",
    )(marks, wanted, payloads)
    return lists, starts[:rows, 0]


def padded_rows(x, rows):
    return jnp.pad(x, ((0, rows - x.shape[0]), (0, 0)))


def pack_pages(core, starts, lists, pieces, own_k, own_v, sib=None):
    count = max(pieces)
    shifts, width = lists.shape
    per_source = own_k.shape[0]
    page = own_k.shape[1:]
    sibs = () if sib is None else sib

    def kernel(core_ref, start_ref, list_ref, ok, ov, *rest):
        sib_refs, rest = rest[: len(sibs)], rest[len(sibs) :]
        outs, (buf, sems, out_sems) = rest[:-3], rest[-3:]

        def outgoing(s):
            for p, piece in enumerate(pieces):
                yield copy(
                    buf.at[s, pl.ds(0, piece)], outs[p * shifts + s], out_sems.at[p * shifts + s]
                )

        def gather(own, other):
            for s in range(shifts):
                start = start_ref[s]

                def body(j, carry, s=s, start=start):
                    i = jnp.maximum(list_ref[s, jnp.minimum(start + j, width - 1)], 0)
                    if other is None:
                        copy(own.at[jnp.minimum(i, per_source - 1)], buf.at[s, j], sems.at[s]).start()
                    else:

                        @pl.when(i < per_source)
                        def _():
                            copy(own.at[i], buf.at[s, j], sems.at[s]).start()

                        @pl.when(i >= per_source)
                        def _():
                            copy(other.at[i - per_source], buf.at[s, j], sems.at[s]).start()

                    return carry

                lax.fori_loop(0, count, body, 0, unroll=4)

        @pl.when(core_ref[0] == 0)
        def _():
            gather(ok, sib_refs[0] if sibs else None)

        @pl.when(core_ref[0] != 0)
        def _():
            gather(ov, sib_refs[1] if sibs else None)

        for s in range(shifts):
            copy(buf.at[s], buf.at[s], sems.at[s]).wait()
            for sent in outgoing(s):
                sent.start()
        for s in range(shifts):
            for sent in outgoing(s):
                sent.wait()

    packed = pl.pallas_call(
        kernel,
        out_shape=[
            jax.ShapeDtypeStruct((piece,) + page, own_k.dtype)
            for piece in pieces
            for _ in range(shifts)
        ],
        in_specs=[SMEM, SMEM, SMEM, ANY, ANY] + [ANY] * len(sibs),
        out_specs=[ANY] * (shifts * len(pieces)),
        scratch_shapes=[
            pltpu.VMEM((shifts, count) + page, own_k.dtype),
            pltpu.SemaphoreType.DMA((shifts,)),
            pltpu.SemaphoreType.DMA((shifts * len(pieces),)),
        ],
        compiler_params=params(),
        cost_estimate=cost(shifts * count * page[0] * page[1] * 8),
        name="pack_pages",
    )(core, starts, lists, own_k, own_v, *sibs)
    return [packed[p * shifts : (p + 1) * shifts] for p in range(len(pieces))]


def settle_local(lists, own, sib, pools):
    count = lists.shape[1]
    per_source = own[0].shape[0]
    page = own[0].shape[1:]

    def kernel(list_ref, *rest):
        sources = (rest[0:2], rest[2:4])
        pk, pv, buf, sem, osem = rest[6:]
        targets = (pk, pv)

        def each(f):
            total = 0
            for who in range(2):

                def body(j, n, who=who):
                    v = list_ref[who, j]

                    @pl.when(v >= 0)
                    def _():
                        f(who, j, v // per_source, v % per_source)

                    return n + jnp.where(v >= 0, 2, 0)

                total = lax.fori_loop(0, count, body, total, unroll=2)
            return total

        def gather(who, j, row, slot):
            for kind in range(2):
                copy(sources[who][kind].at[row], buf.at[kind, who, j], sem).start()

        def scatter(who, j, row, slot):
            for kind in range(2):
                copy(buf.at[kind, who, j], targets[kind].at[slot], osem).start()

        def drain(a_sem):
            def body(j, carry):
                copy(buf.at[0, 0, 0], pk.at[0], a_sem).wait()
                return carry

            return body

        lax.fori_loop(0, each(gather), drain(sem), 0)
        lax.fori_loop(0, each(scatter), drain(osem), 0)

    shape = jax.ShapeDtypeStruct(own[0].shape, own[0].dtype)
    return pl.pallas_call(
        kernel,
        out_shape=[shape, shape],
        in_specs=[SMEM] + [ANY] * 6,
        out_specs=[ANY, ANY],
        input_output_aliases={5: 0, 6: 1},
        scratch_shapes=[
            pltpu.VMEM((2, 2, count) + page, own[0].dtype),
            pltpu.SemaphoreType.DMA,
            pltpu.SemaphoreType.DMA,
        ],
        compiler_params=params(),
        cost_estimate=cost(count * page[0] * page[1] * 32),
        name="settle_local",
    )(lists, *own, *sib, *pools)


def settle_pages(core, spans, lists, direct, swapped, per_source, pools=()):
    shifts = len(direct[0])
    pieces = [piece[0].shape[0] for piece in direct]
    n_arrays = shifts * len(pieces)
    page = direct[0][0].shape[1:]
    width = lists.shape[1]

    def kernel(core_ref, span_ref, list_ref, *rest):
        arrived = (rest[:n_arrays], rest[n_arrays : 2 * n_arrays])
        pk, pv, buf, sems, osem = rest[2 * n_arrays + len(pools) :]
        low = core_ref[0] * per_source

        def incoming(k, p, s):
            where = pl.ds(sum(pieces[:p]), pieces[p])
            i = p * shifts + s
            return copy(arrived[k][i], buf.at[k, s, where], sems.at[k, i])

        order = [
            (k, p, s) for s in range(shifts) for k in range(2) for p in range(len(pieces))
        ]
        for k, p, s in order:
            incoming(k, p, s).start()

        def scatter(targets):
            total = 0
            for k, p, s in order:
                incoming(k, p, s).wait()
                if p + 1 < len(pieces):
                    continue
                row = k * shifts + s
                start, limit = span_ref[row, 0], span_ref[row, 1]

                def body(j, n, s=s, k=k, row=row, start=start, limit=limit):
                    place = start + j
                    slot = list_ref[row, jnp.minimum(place, width - 1)] - low
                    mine = (slot >= 0) & (slot < per_source) & (place < limit)

                    @pl.when(mine)
                    def _():
                        copy(buf.at[k, s, j], targets[k].at[slot], osem).start()

                    return n + jnp.where(mine, 1, 0)

                total = lax.fori_loop(0, sum(pieces), body, total, unroll=4)

            def drain(j, carry):
                copy(buf.at[0, 0, 0], targets[0].at[0], osem).wait()
                return carry

            lax.fori_loop(0, total, drain, 0)

        @pl.when(core_ref[0] == 0)
        def _():
            scatter((pk, pv))

        @pl.when(core_ref[0] != 0)
        def _():
            scatter((pv, pk))

    dtype = direct[0][0].dtype
    shape = jax.ShapeDtypeStruct((per_source,) + page, dtype)
    first = 3 + 2 * n_arrays
    return pl.pallas_call(
        kernel,
        out_shape=[shape, shape],
        in_specs=[SMEM, SMEM, SMEM] + [ANY] * (2 * n_arrays + len(pools)),
        out_specs=[ANY, ANY],
        input_output_aliases={first: 0, first + 1: 1} if pools else {},
        scratch_shapes=[
            pltpu.VMEM((2, shifts, sum(pieces)) + page, dtype),
            pltpu.SemaphoreType.DMA((2, n_arrays)),
            pltpu.SemaphoreType.DMA,
        ],
        compiler_params=params(),
        cost_estimate=cost(shifts * sum(pieces) * page[0] * page[1] * 16),
        name="settle_pages",
    )(core, spans, lists, *sum(direct, []), *sum(swapped, []), *pools)


def bounds_of(row_of, queries, pages, block, ahead=None):
    n_pages, page_rows, width = pages.shape
    rows = queries.shape[0]
    kv_local = width // HD
    heads = queries.shape[1] // HD
    group = heads // kv_local
    scale = 1.0 / math.sqrt(HD)
    steps = n_pages // block
    before = 0 if ahead is None else ahead.shape[1]

    def kernel(row_ref, q_ref, page_ref, *rest):
        out_ref, parts = rest[-2:]
        x = page_ref[...]
        low = jnp.min(x, axis=1)
        high = jnp.max(x, axis=1)
        owner = row_ref[...]
        results = []
        for h in range(kv_local):
            part = slice(h * HD, (h + 1) * HD)
            result = jnp.zeros((group, block), jnp.float32)
            for r in range(rows):
                q = q_ref[r, h * group : (h + 1) * group, :]
                zero = jnp.zeros_like(q)
                dims = (((1,), (1,)), ((), ()))
                both = lax.dot_general(
                    jnp.maximum(q, zero), high[:, part], dims, preferred_element_type=jnp.float32
                ) + lax.dot_general(
                    jnp.minimum(q, zero), low[:, part], dims, preferred_element_type=jnp.float32
                )
                result = jnp.where(owner == r, both, result)
            results.append(result * scale)
        parts[pl.program_id(0)] = jnp.concatenate(results)

        @pl.when(pl.program_id(0) == steps - 1)
        def _():
            done = [rest[0][...]] if before else []
            out_ref[...] = jnp.concatenate(done + [parts[i] for i in range(steps)], axis=1)

    return pl.pallas_call(
        kernel,
        grid=(steps,),
        out_shape=jax.ShapeDtypeStruct((heads, before + n_pages), jnp.float32),
        in_specs=[
            pl.BlockSpec((1, block), lambda i: (0, i)),
            pl.BlockSpec((rows, heads, HD), lambda i: (0, 0, 0)),
            pl.BlockSpec((block, page_rows, width), lambda i: (i, 0, 0)),
        ]
        + ([pl.BlockSpec((heads, before), lambda i: (0, 0))] if before else []),
        out_specs=pl.BlockSpec((heads, before + n_pages), lambda i: (0, 0)),
        scratch_shapes=[pltpu.VMEM((steps, heads, block), jnp.float32)],
        compiler_params=params(),
        name="bounds",
    )(row_of, queries.reshape(rows, heads, HD), pages, *([ahead] if before else []))


def attend(page_slots, live, queries, self_keys, self_values, res_k, res_v, pool_k, pool_v):
    rows, k_sel = page_slots.shape
    res_count, page_rows, width = res_k.shape
    kv_local = width // HD
    heads = queries.shape[1] // HD
    group = heads // kv_local
    tokens = k_sel * page_rows
    scale = 1.0 / math.sqrt(HD)

    def kernel(slot_ref, live_ref, q_ref, sk_ref, sv_ref, rk, rv, pk, pv, out_ref, kb, vb, sems):
        for r in range(rows):

            def body(j, carry, r=r):
                slot = slot_ref[r, j]

                @pl.when(slot < res_count)
                def _():
                    copy(rk.at[slot], kb.at[r, j], sems.at[r, 0]).start()
                    copy(rv.at[slot], vb.at[r, j], sems.at[r, 1]).start()

                @pl.when(slot >= res_count)
                def _():
                    copy(pk.at[slot - res_count], kb.at[r, j], sems.at[r, 0]).start()
                    copy(pv.at[slot - res_count], vb.at[r, j], sems.at[r, 1]).start()

                return carry

            lax.fori_loop(0, k_sel, body, 0)
        for r in range(rows):
            copy(kb.at[r], kb.at[r], sems.at[r, 0]).wait()
            copy(vb.at[r], vb.at[r], sems.at[r, 1]).wait()
            alive = live_ref[r : r + 1, :] > 0
            for h in range(kv_local):
                part = slice(h * HD, (h + 1) * HD)
                here = slice(h * group, (h + 1) * group)
                q = q_ref[r, here, :]
                keys = kb[r, :, :, part].reshape(tokens, HD)
                values = vb[r, :, :, part].reshape(tokens, HD)
                scores = (
                    lax.dot_general(
                        q, keys, (((1,), (1,)), ((), ())), preferred_element_type=jnp.float32
                    )
                    * scale
                )
                scores = jnp.where(alive, scores, -1e30)
                self_key = sk_ref[r : r + 1, part].astype(jnp.float32)
                self_score = (
                    jnp.sum(q.astype(jnp.float32) * self_key, axis=1, keepdims=True) * scale
                )
                top = jnp.maximum(jnp.max(scores, axis=1, keepdims=True), self_score)
                weights = jnp.where(alive, jnp.exp(scores - top), 0.0)
                self_weight = jnp.exp(self_score - top)
                total = jnp.sum(weights, axis=1, keepdims=True) + self_weight
                mixed = lax.dot_general(
                    weights.astype(jnp.bfloat16),
                    values,
                    (((1,), (0,)), ((), ())),
                    preferred_element_type=jnp.float32,
                )
                self_rounded = self_weight.astype(jnp.bfloat16).astype(jnp.float32)
                mixed = mixed + self_rounded * sv_ref[r : r + 1, part].astype(jnp.float32)
                out_ref[r, here, :] = (mixed / total).astype(jnp.bfloat16)

    return pl.pallas_call(
        kernel,
        out_shape=jax.ShapeDtypeStruct((rows, heads, HD), jnp.bfloat16),
        in_specs=[SMEM, VMEM, VMEM, VMEM, VMEM, ANY, ANY, ANY, ANY],
        out_specs=VMEM,
        scratch_shapes=[
            pltpu.VMEM((rows, k_sel, page_rows, width), jnp.bfloat16),
            pltpu.VMEM((rows, k_sel, page_rows, width), jnp.bfloat16),
            pltpu.SemaphoreType.DMA((rows, 2)),
        ],
        compiler_params=params(),
        name="attend",
    )(
        page_slots,
        live,
        queries.reshape(rows, heads, HD),
        self_keys,
        self_values,
        res_k,
        res_v,
        pool_k,
        pool_v,
    )


def project(partial):
    ranks = lax.axis_size("head")
    here = lax.axis_index("head")
    columns = partial.shape[1] // ranks

    def piece(owner):
        return lax.dynamic_slice_in_dim(partial, owner * columns, columns, 1)

    total = piece(here)
    for s in range(1, ranks):
        pairs = [(k, (k + s) % ranks) for k in range(ranks)]
        total = total + lax.ppermute(piece((here + s) % ranks), "head", pairs)
    return total.astype(jnp.bfloat16)


def on_device(
    new_keys,
    new_values,
    page_dest,
    page_slot,
    resident_keys,
    resident_values,
    queries,
    self_keys,
    self_values,
    context_len,
    selected,
    out_weight,
):
    groups = lax.axis_size("grp")
    chips = groups // CORES
    me = lax.axis_index("grp")
    chip, core = me // CORES, me % CORES
    per_source, page_rows = new_keys.shape[:2]
    res_count = resident_keys.shape[0]
    rows_here = queries.shape[0]
    pair_cap = 2 * per_source // groups
    cap = CORES * CORES * pair_cap
    unit = cap // 16
    first, second, third = 3 * unit, 4 * unit, 7 * unit // 2
    shifts = chips - 1

    def permute(x, shift):
        return lax.ppermute(x, "grp", [(i, i ^ shift) for i in range(groups)])

    def after(x, *others):
        return lax.optimization_barrier((x, *others))[0]

    def send(packed):
        return [[permute(x, (s + 1) * CORES) for s, x in enumerate(piece)] for piece in packed]

    me_list, core_list = me.reshape(1), core.reshape(1)
    own_ids = jnp.arange(per_source, dtype=jnp.int32)
    width = cap + 8

    page_counts = (context_len + page_rows - 1) // page_rows
    row_end = jnp.cumsum(page_counts)
    row_start = row_end - page_counts
    page_slots = row_start[:, None] + selected
    chosen = (page_slots.reshape(-1, 1) - res_count == own_ids[None, :]).astype(jnp.int32)
    chosen = jnp.max(chosen, axis=0)

    own_info = jnp.stack([page_dest, page_slot, chosen])
    infos = jnp.stack([own_info] + [permute(own_info, s * CORES) for s in range(1, chips)])
    infos = jnp.stack([infos, permute(infos, 1)], axis=1)
    dest, slot, flags = infos[:, :, 0], infos[:, :, 1], infos[:, :, 2]
    flags = flags.reshape(groups, per_source)

    own_sends = first_lists(me_list, page_dest[None], shifts, first)
    packed = pack_pages(
        core_list, jnp.zeros((shifts,), jnp.int32), own_sends, [first], new_keys, new_values
    )
    direct0 = send(packed)

    dest, slot = lax.optimization_barrier((dest, slot, packed))[:2]
    away = dest ^ me
    padded = -(-shifts // 8) * 8
    shift_ids = jnp.arange(1, padded + 1, dtype=jnp.int32)
    chip_away = (away[0] // CORES).reshape(1, -1)
    wanted = wanted_of(away[0], slot[0], flags).reshape(1, -1)
    ids = jnp.arange(CORES * per_source, dtype=jnp.int32)[None]
    sends, send_start = full_lists(
        (chip_away == shift_ids[:, None]).astype(jnp.int32),
        jnp.broadcast_to(wanted, (padded, wanted.shape[1])),
        jnp.broadcast_to(ids, (padded, ids.shape[1])),
        shifts,
        per_source,
        first,
        width,
    )

    new_keys_, new_values_ = lax.optimization_barrier((new_keys, new_values, packed))[:2]
    sib = (permute(new_keys_, 1), permute(new_values_, 1))

    def pack(offset, pieces, start=send_start):
        return pack_pages(core_list, start + offset, sends, pieces, new_keys, new_values, sib)

    packed = pack(0, [second])
    dest, slot = lax.optimization_barrier((dest, slot, packed))[:2]

    chip_ids = jnp.arange(chips, dtype=jnp.int32)
    counts = jnp.sum((dest[..., None] // CORES == chip_ids).astype(jnp.int32), axis=2)
    late = jnp.sum(counts, axis=1, keepdims=True) - jnp.minimum(counts, first)
    late = jnp.where((chip ^ chip_ids)[:, None, None] == chip_ids[None, None, :], 0, late)
    needed = jnp.max(late)

    def both_kinds(x):
        x = jnp.concatenate([x[1:], x[1:, ::-1]]).reshape(2 * shifts, -1)
        return padded_rows(x, -(-2 * shifts // 8) * 8)

    arrive_wanted = wanted_of(
        (dest ^ me)[1:].reshape(shifts * CORES, -1), slot[1:].reshape(shifts * CORES, -1), flags
    ).reshape(shifts, CORES, -1)
    arrive_wanted = jnp.concatenate([wanted.reshape(1, CORES, -1), arrive_wanted])
    to_chip = (dest[..., None] // CORES == chip_ids).astype(jnp.float32)
    most_wanted = jnp.max(jnp.sum(arrive_wanted[..., None] * to_chip, axis=(1, 2)))
    soon = most_wanted <= second
    arrivals, arrive_start = full_lists(
        both_kinds((dest // CORES == chip).astype(jnp.int32)),
        both_kinds(arrive_wanted),
        both_kinds((dest % CORES) * per_source + slot),
        2 * shifts,
        per_source,
        first,
        width,
    )

    packed, direct0, dest, slot, arrivals, arrive_start = lax.optimization_barrier(
        (packed, direct0, dest, slot, arrivals, arrive_start)
    )
    direct1 = send(packed)

    def spans_at(arrive_start, offset):
        start = arrive_start + offset
        return jnp.stack([start, jnp.full_like(start, width)], axis=1)

    early_spans = jnp.stack([jnp.zeros_like(arrive_start), arrive_start], axis=1)

    def settle(spans, direct, pools=()):
        swapped = [[permute(x, 1) for x in piece] for piece in direct]
        return settle_pages(core_list, spans, arrivals, direct, swapped, per_source, pools)

    slot_ids = jnp.arange(res_count + per_source, dtype=jnp.int32)
    owner_row = jnp.sum((slot_ids[None, :] >= row_end[:, None]).astype(jnp.int32), axis=0)[None]
    res_bounds = bounds_of(
        owner_row[:, :res_count], queries, after(resident_keys, packed), res_count
    )
    pools = settle(early_spans, direct0)

    locals_ = invert(
        jnp.stack([dest[0, 0] == me, dest[0, 1] == me]),
        own_ids[None, :] * per_source + slot[0],
        pair_cap,
    )

    held = [unit // 2, unit, 2 * unit, 3 * unit]
    packed, kept, direct1, pools, res_bounds, locals_ = lax.optimization_barrier(
        (
            pack(second, [third]),
            pack(second + third, held),
            direct1,
            pools,
            res_bounds,
            locals_,
        )
    )
    direct2 = send(packed)
    pools = settle_local(locals_, (new_keys, new_values), sib, pools)
    pools = settle(spans_at(arrive_start, 0), direct1, pools)

    within = jnp.arange(page_rows, dtype=jnp.int32)
    live = (
        (selected[:, :, None] * page_rows + within[None, None, :] < context_len[:, None, None])
        .astype(jnp.int32)
        .reshape(rows_here, -1)
    )

    def decode(pools):
        attended = attend(
            page_slots,
            live,
            queries,
            self_keys,
            self_values,
            resident_keys,
            resident_values,
            *pools,
        )
        return project(
            jnp.dot(attended.reshape(rows_here, -1), out_weight, preferred_element_type=jnp.float32)
        )

    projected = decode(pools)

    kept, direct2, pools, needed, soon, projected, info = lax.optimization_barrier(
        (
            kept,
            direct2,
            pools,
            needed,
            soon,
            projected,
            (send_start, arrive_start),
        )
    )

    def rest(total):
        def branch(ops):
            kept, direct, pools, (send_start, arrive_start) = ops
            arrived = []
            if total:
                arrived = send([kept[held.index(min(total, held[-1]))]])
            pools = settle(spans_at(arrive_start, second), direct, pools)
            if total > held[-1]:
                late = pack(second + third + held[-1], [total - held[-1]], send_start)
                arrived = arrived + send(late)
            pools, arrived = lax.optimization_barrier((pools, arrived))
            if arrived:
                pools = settle(spans_at(arrive_start, second + third), arrived, pools)
            return pools

        return branch

    totals = [0] + held + [held[-1] + k * unit for k in (1, 2)] + [cap - second - third]
    left = needed - second - third
    which = sum((left > total).astype(jnp.int32) for total in totals[:-1])
    ops = (kept, direct2, pools, info)
    if chips <= 4:
        pools = lax.switch(which, [rest(total) for total in totals], ops)
    else:
        pools = rest(totals[-1])(ops)
    pool_k, pool_v = pools
    projected = lax.cond(soon, lambda pools: projected, decode, pools)

    slot_bounds = bounds_of(
        owner_row[:, res_count:], queries, pool_k, min(128, per_source), res_bounds
    )
    return pool_k, pool_v, slot_bounds, projected


def solution(mesh):
    in_specs = (
        P("grp", None, "head"),
        P("grp", None, "head"),
        P("grp"),
        P("grp"),
        P("grp", None, "head"),
        P("grp", None, "head"),
        P("grp", "head"),
        P("grp", "head"),
        P("grp", "head"),
        P("grp"),
        P("grp", None),
        P("head", None),
    )
    out_specs = (P("grp", None, "head"), P("grp", None, "head"), P("head", "grp"), P("grp", "head"))
    return jax.shard_map(
        on_device, mesh=mesh, in_specs=in_specs, out_specs=out_specs, check_vma=False
    )
```

```python
import functools
import math

import jax
import jax.numpy as jnp
from jax import lax
from jax.experimental import pallas as pl
from jax.experimental.pallas import tpu as pltpu
from jax.sharding import PartitionSpec as P

HD = 128
CORES = 2
ANY = pl.BlockSpec(memory_space=pl.ANY)
SMEM = pl.BlockSpec(memory_space=pltpu.SMEM)
VMEM = pl.BlockSpec(memory_space=pltpu.VMEM)
VMEM_LIMIT = 26 << 20


def params(**kw):
    return pltpu.CompilerParams(vmem_limit_bytes=VMEM_LIMIT, **kw)


def cost(size):
    return pl.CostEstimate(flops=0, bytes_accessed=size // 64, transcendentals=0)


def copy(src, dst, sem):
    return pltpu.make_async_copy(src, dst, sem)


def invert(marks, payloads, width):
    rows, size = marks.shape
    padded = -(-rows // 8) * 8
    marks = jnp.pad(marks.astype(jnp.int32), ((0, padded - rows), (0, 0)))
    payloads = jnp.pad(payloads, ((0, padded - rows), (0, 0)))

    def kernel(mark_ref, payload_ref, out_ref):
        marked = mark_ref[...]
        upto = (
            lax.broadcasted_iota(jnp.int32, (size, size), 0)
            <= lax.broadcasted_iota(jnp.int32, (size, size), 1)
        ).astype(jnp.float32)
        ranks = jnp.dot(
            marked.astype(jnp.float32).astype(jnp.bfloat16),
            upto.astype(jnp.bfloat16),
            preferred_element_type=jnp.float32,
        )
        ranks = jnp.where(marked > 0, ranks - 1.0, -1.0).astype(jnp.int32)
        places = lax.broadcasted_iota(jnp.int32, (width, size), 0)
        parts = lax.broadcasted_iota(jnp.int32, (8, size), 0)
        for t in range(rows):
            hits = (ranks[t : t + 1, :] == places).astype(jnp.float32).astype(jnp.bfloat16)
            value = payload_ref[t : t + 1, :]
            pieces = jnp.where(parts < 3, (value >> (7 * jnp.minimum(parts, 2))) & 127, 1)
            found = lax.dot_general(
                pieces.astype(jnp.float32).astype(jnp.bfloat16),
                hits,
                (((1,), (1,)), ((), ())),
                preferred_element_type=jnp.float32,
            ).astype(jnp.int32)
            whole = found[0:1] + found[1:2] * 128 + found[2:3] * 16384
            out_ref[t : t + 1, :] = jnp.where(found[3:4] > 0, whole, -1)

    return pl.pallas_call(
        kernel,
        out_shape=jax.ShapeDtypeStruct((rows, width), jnp.int32),
        in_specs=[VMEM, VMEM],
        out_specs=VMEM,
        compiler_params=params(),
        name="invert",
    )(marks, payloads)


def triangle(size):
    row = lax.broadcasted_iota(jnp.int32, (size, size), 0)
    column = lax.broadcasted_iota(jnp.int32, (size, size), 1)
    return (row <= column).astype(jnp.float32).astype(jnp.bfloat16)


def running(marks, upto):
    return jnp.dot(marks.astype(jnp.bfloat16), upto, preferred_element_type=jnp.float32)


def place(rank_row, payload_row, width):
    size = rank_row.shape[1]
    places = lax.broadcasted_iota(jnp.int32, (width, size), 0)
    hits = (rank_row.astype(jnp.int32) == places).astype(jnp.float32).astype(jnp.bfloat16)
    parts = lax.broadcasted_iota(jnp.int32, (8, size), 0)
    pieces = jnp.where(parts < 2, (payload_row >> (7 * jnp.minimum(parts, 1))) & 127, 1)
    found = lax.dot_general(
        pieces.astype(jnp.float32).astype(jnp.bfloat16),
        hits,
        (((1,), (1,)), ((), ())),
        preferred_element_type=jnp.float32,
    ).astype(jnp.int32)
    return jnp.where(found[2:3] > 0, found[0:1] + found[1:2] * 128, -1)


def first_lists(me, dest, shifts, width):
    size = dest.shape[1]
    padded = -(-shifts // 8) * 8

    def kernel(me_ref, dest_ref, out_ref):
        away = (dest_ref[...] ^ me_ref[0]) // CORES
        shift = lax.broadcasted_iota(jnp.int32, (padded, size), 0) + 1
        marks = (away == shift).astype(jnp.float32)
        ranks = jnp.where(marks > 0, running(marks, triangle(size)) - 1.0, -1.0)
        ids = lax.broadcasted_iota(jnp.int32, (1, size), 1)
        for t in range(shifts):
            out_ref[t : t + 1, :] = place(ranks[t : t + 1, :], ids, width)

    return pl.pallas_call(
        kernel,
        out_shape=jax.ShapeDtypeStruct((shifts, width), jnp.int32),
        in_specs=[SMEM, VMEM],
        out_specs=VMEM,
        compiler_params=params(),
        name="first_lists",
    )(me, dest)


def wanted_of(owner, slot, flags):
    rows, size = slot.shape
    owners, slots = flags.shape

    def kernel(owner_ref, slot_ref, flag_ref, out_ref):
        flag = flag_ref[...].astype(jnp.float32).astype(jnp.bfloat16)
        for r in range(rows):
            spot = lax.broadcasted_iota(jnp.int32, (slots, size), 0)
            hits = (slot_ref[r : r + 1, :] == spot).astype(jnp.float32).astype(jnp.bfloat16)
            found = jnp.dot(flag, hits, preferred_element_type=jnp.float32)
            who = lax.broadcasted_iota(jnp.int32, (owners, size), 0)
            out_ref[r : r + 1, :] = jnp.sum(
                jnp.where(owner_ref[r : r + 1, :] == who, found, 0.0), axis=0, keepdims=True
            )

    return pl.pallas_call(
        kernel,
        out_shape=jax.ShapeDtypeStruct((rows, size), jnp.float32),
        in_specs=[VMEM, VMEM, VMEM],
        out_specs=VMEM,
        compiler_params=params(),
        name="wanted_of",
    )(owner, slot, flags)


def full_lists(marks, wanted, payloads, rows, own, first, width):
    padded, size = marks.shape

    def kernel(mark_ref, want_ref, payload_ref, out_ref, start_ref):
        upto = triangle(size)
        marks = mark_ref[...].astype(jnp.float32)
        want = want_ref[...]
        count = running(marks, upto)
        column = lax.broadcasted_iota(jnp.int32, (padded, size), 1)
        early = jnp.where((column < own) & (count <= first), marks, 0.0)
        wanted = (marks - early) * want
        others = (marks - early) * (1.0 - want)
        n_early = jnp.sum(early, axis=1, keepdims=True)
        n_wanted = jnp.sum(wanted, axis=1, keepdims=True)
        ranks = jnp.where(
            early > 0,
            count - 1.0,
            jnp.where(
                wanted > 0,
                n_early + running(wanted, upto) - 1.0,
                jnp.where(others > 0, n_early + n_wanted + running(others, upto) - 1.0, -1.0),
            ),
        )
        start_ref[...] = jnp.broadcast_to(n_early, start_ref.shape).astype(jnp.int32)
        for t in range(rows):
            out_ref[t : t + 1, :] = place(
                ranks[t : t + 1, :], payload_ref[t : t + 1, :], width
            )

    lists, starts = pl.pallas_call(
        kernel,
        out_shape=[
            jax.ShapeDtypeStruct((rows, width), jnp.int32),
            jax.ShapeDtypeStruct((padded, 128), jnp.int32),
        ],
        in_specs=[VMEM, VMEM, VMEM],
        out_specs=[VMEM, VMEM],
        compiler_params=params(),
        name="full_lists",
    )(marks, wanted, payloads)
    return lists, starts[:rows, 0]


def padded_rows(x, rows):
    return jnp.pad(x, ((0, rows - x.shape[0]), (0, 0)))


def pack_pages(core, starts, lists, pieces, own_k, own_v, sib=None):
    count = max(pieces)
    shifts, width = lists.shape
    per_source = own_k.shape[0]
    page = own_k.shape[1:]
    sibs = () if sib is None else sib

    def kernel(core_ref, start_ref, list_ref, ok, ov, *rest):
        sib_refs, rest = rest[: len(sibs)], rest[len(sibs) :]
        outs, (buf, sems, out_sems) = rest[:-3], rest[-3:]

        def outgoing(s):
            for p, piece in enumerate(pieces):
                yield copy(
                    buf.at[s, pl.ds(0, piece)], outs[p * shifts + s], out_sems.at[p * shifts + s]
                )

        def gather(own, other):
            for s in range(shifts):
                start = start_ref[s]

                def body(j, carry, s=s, start=start):
                    i = jnp.maximum(list_ref[s, jnp.minimum(start + j, width - 1)], 0)
                    if other is None:
                        copy(own.at[jnp.minimum(i, per_source - 1)], buf.at[s, j], sems.at[s]).start()
                    else:

                        @pl.when(i < per_source)
                        def _():
                            copy(own.at[i], buf.at[s, j], sems.at[s]).start()

                        @pl.when(i >= per_source)
                        def _():
                            copy(other.at[i - per_source], buf.at[s, j], sems.at[s]).start()

                    return carry

                lax.fori_loop(0, count, body, 0, unroll=4)

        @pl.when(core_ref[0] == 0)
        def _():
            gather(ok, sib_refs[0] if sibs else None)

        @pl.when(core_ref[0] != 0)
        def _():
            gather(ov, sib_refs[1] if sibs else None)

        for s in range(shifts):
            copy(buf.at[s], buf.at[s], sems.at[s]).wait()
            for sent in outgoing(s):
                sent.start()
        for s in range(shifts):
            for sent in outgoing(s):
                sent.wait()

    packed = pl.pallas_call(
        kernel,
        out_shape=[
            jax.ShapeDtypeStruct((piece,) + page, own_k.dtype)
            for piece in pieces
            for _ in range(shifts)
        ],
        in_specs=[SMEM, SMEM, SMEM, ANY, ANY] + [ANY] * len(sibs),
        out_specs=[ANY] * (shifts * len(pieces)),
        scratch_shapes=[
            pltpu.VMEM((shifts, count) + page, own_k.dtype),
            pltpu.SemaphoreType.DMA((shifts,)),
            pltpu.SemaphoreType.DMA((shifts * len(pieces),)),
        ],
        compiler_params=params(),
        cost_estimate=cost(shifts * count * page[0] * page[1] * 8),
        name="pack_pages",
    )(core, starts, lists, own_k, own_v, *sibs)
    return [packed[p * shifts : (p + 1) * shifts] for p in range(len(pieces))]


def settle_local(lists, own, sib, pools):
    count = lists.shape[1]
    per_source = own[0].shape[0]
    page = own[0].shape[1:]

    def kernel(list_ref, *rest):
        sources = (rest[0:2], rest[2:4])
        pk, pv, buf, sem, osem = rest[6:]
        targets = (pk, pv)

        def each(f):
            total = 0
            for who in range(2):

                def body(j, n, who=who):
                    v = list_ref[who, j]

                    @pl.when(v >= 0)
                    def _():
                        f(who, j, v // per_source, v % per_source)

                    return n + jnp.where(v >= 0, 2, 0)

                total = lax.fori_loop(0, count, body, total, unroll=2)
            return total

        def gather(who, j, row, slot):
            for kind in range(2):
                copy(sources[who][kind].at[row], buf.at[kind, who, j], sem).start()

        def scatter(who, j, row, slot):
            for kind in range(2):
                copy(buf.at[kind, who, j], targets[kind].at[slot], osem).start()

        def drain(a_sem):
            def body(j, carry):
                copy(buf.at[0, 0, 0], pk.at[0], a_sem).wait()
                return carry

            return body

        lax.fori_loop(0, each(gather), drain(sem), 0)
        lax.fori_loop(0, each(scatter), drain(osem), 0)

    shape = jax.ShapeDtypeStruct(own[0].shape, own[0].dtype)
    return pl.pallas_call(
        kernel,
        out_shape=[shape, shape],
        in_specs=[SMEM] + [ANY] * 6,
        out_specs=[ANY, ANY],
        input_output_aliases={5: 0, 6: 1},
        scratch_shapes=[
            pltpu.VMEM((2, 2, count) + page, own[0].dtype),
            pltpu.SemaphoreType.DMA,
            pltpu.SemaphoreType.DMA,
        ],
        compiler_params=params(),
        cost_estimate=cost(count * page[0] * page[1] * 32),
        name="settle_local",
    )(lists, *own, *sib, *pools)


def settle_pages(core, spans, lists, direct, swapped, per_source, pools=()):
    shifts = len(direct[0])
    pieces = [piece[0].shape[0] for piece in direct]
    n_arrays = shifts * len(pieces)
    page = direct[0][0].shape[1:]
    width = lists.shape[1]

    def kernel(core_ref, span_ref, list_ref, *rest):
        arrived = (rest[:n_arrays], rest[n_arrays : 2 * n_arrays])
        pk, pv, buf, sems, osem = rest[2 * n_arrays + len(pools) :]
        low = core_ref[0] * per_source

        def incoming(k, p, s):
            where = pl.ds(sum(pieces[:p]), pieces[p])
            i = p * shifts + s
            return copy(arrived[k][i], buf.at[k, s, where], sems.at[k, i])

        order = [
            (k, p, s) for s in range(shifts) for k in range(2) for p in range(len(pieces))
        ]
        for k, p, s in order:
            incoming(k, p, s).start()

        def scatter(targets):
            total = 0
            for k, p, s in order:
                incoming(k, p, s).wait()
                if p + 1 < len(pieces):
                    continue
                row = k * shifts + s
                start, limit = span_ref[row, 0], span_ref[row, 1]

                def body(j, n, s=s, k=k, row=row, start=start, limit=limit):
                    place = start + j
                    slot = list_ref[row, jnp.minimum(place, width - 1)] - low
                    mine = (slot >= 0) & (slot < per_source) & (place < limit)

                    @pl.when(mine)
                    def _():
                        copy(buf.at[k, s, j], targets[k].at[slot], osem).start()

                    return n + jnp.where(mine, 1, 0)

                total = lax.fori_loop(0, sum(pieces), body, total, unroll=4)

            def drain(j, carry):
                copy(buf.at[0, 0, 0], targets[0].at[0], osem).wait()
                return carry

            lax.fori_loop(0, total, drain, 0)

        @pl.when(core_ref[0] == 0)
        def _():
            scatter((pk, pv))

        @pl.when(core_ref[0] != 0)
        def _():
            scatter((pv, pk))

    dtype = direct[0][0].dtype
    shape = jax.ShapeDtypeStruct((per_source,) + page, dtype)
    first = 3 + 2 * n_arrays
    return pl.pallas_call(
        kernel,
        out_shape=[shape, shape],
        in_specs=[SMEM, SMEM, SMEM] + [ANY] * (2 * n_arrays + len(pools)),
        out_specs=[ANY, ANY],
        input_output_aliases={first: 0, first + 1: 1} if pools else {},
        scratch_shapes=[
            pltpu.VMEM((2, shifts, sum(pieces)) + page, dtype),
            pltpu.SemaphoreType.DMA((2, n_arrays)),
            pltpu.SemaphoreType.DMA,
        ],
        compiler_params=params(),
        cost_estimate=cost(shifts * sum(pieces) * page[0] * page[1] * 16),
        name="settle_pages",
    )(core, spans, lists, *sum(direct, []), *sum(swapped, []), *pools)


def bounds_of(row_of, queries, pages, block, ahead=None):
    n_pages, page_rows, width = pages.shape
    rows = queries.shape[0]
    kv_local = width // HD
    heads = queries.shape[1] // HD
    group = heads // kv_local
    scale = 1.0 / math.sqrt(HD)
    steps = n_pages // block
    before = 0 if ahead is None else ahead.shape[1]

    def kernel(row_ref, q_ref, page_ref, *rest):
        out_ref, parts = rest[-2:]
        x = page_ref[...]
        low = jnp.min(x, axis=1)
        high = jnp.max(x, axis=1)
        owner = row_ref[...]
        results = []
        for h in range(kv_local):
            part = slice(h * HD, (h + 1) * HD)
            result = jnp.zeros((group, block), jnp.float32)
            for r in range(rows):
                q = q_ref[r, h * group : (h + 1) * group, :]
                zero = jnp.zeros_like(q)
                dims = (((1,), (1,)), ((), ()))
                both = lax.dot_general(
                    jnp.maximum(q, zero), high[:, part], dims, preferred_element_type=jnp.float32
                ) + lax.dot_general(
                    jnp.minimum(q, zero), low[:, part], dims, preferred_element_type=jnp.float32
                )
                result = jnp.where(owner == r, both, result)
            results.append(result * scale)
        parts[pl.program_id(0)] = jnp.concatenate(results)

        @pl.when(pl.program_id(0) == steps - 1)
        def _():
            done = [rest[0][...]] if before else []
            out_ref[...] = jnp.concatenate(done + [parts[i] for i in range(steps)], axis=1)

    return pl.pallas_call(
        kernel,
        grid=(steps,),
        out_shape=jax.ShapeDtypeStruct((heads, before + n_pages), jnp.float32),
        in_specs=[
            pl.BlockSpec((1, block), lambda i: (0, i)),
            pl.BlockSpec((rows, heads, HD), lambda i: (0, 0, 0)),
            pl.BlockSpec((block, page_rows, width), lambda i: (i, 0, 0)),
        ]
        + ([pl.BlockSpec((heads, before), lambda i: (0, 0))] if before else []),
        out_specs=pl.BlockSpec((heads, before + n_pages), lambda i: (0, 0)),
        scratch_shapes=[pltpu.VMEM((steps, heads, block), jnp.float32)],
        compiler_params=params(),
        name="bounds",
    )(row_of, queries.reshape(rows, heads, HD), pages, *([ahead] if before else []))


def attend(page_slots, live, queries, self_keys, self_values, res_k, res_v, pool_k, pool_v):
    rows, k_sel = page_slots.shape
    res_count, page_rows, width = res_k.shape
    kv_local = width // HD
    heads = queries.shape[1] // HD
    group = heads // kv_local
    tokens = k_sel * page_rows
    scale = 1.0 / math.sqrt(HD)

    def kernel(slot_ref, live_ref, q_ref, sk_ref, sv_ref, rk, rv, pk, pv, out_ref, kb, vb, sems):
        for r in range(rows):

            def body(j, carry, r=r):
                slot = slot_ref[r, j]

                @pl.when(slot < res_count)
                def _():
                    copy(rk.at[slot], kb.at[r, j], sems.at[r, 0]).start()
                    copy(rv.at[slot], vb.at[r, j], sems.at[r, 1]).start()

                @pl.when(slot >= res_count)
                def _():
                    copy(pk.at[slot - res_count], kb.at[r, j], sems.at[r, 0]).start()
                    copy(pv.at[slot - res_count], vb.at[r, j], sems.at[r, 1]).start()

                return carry

            lax.fori_loop(0, k_sel, body, 0)
        for r in range(rows):
            copy(kb.at[r], kb.at[r], sems.at[r, 0]).wait()
            copy(vb.at[r], vb.at[r], sems.at[r, 1]).wait()
            alive = live_ref[r : r + 1, :] > 0
            for h in range(kv_local):
                part = slice(h * HD, (h + 1) * HD)
                here = slice(h * group, (h + 1) * group)
                q = q_ref[r, here, :]
                keys = kb[r, :, :, part].reshape(tokens, HD)
                values = vb[r, :, :, part].reshape(tokens, HD)
                scores = (
                    lax.dot_general(
                        q, keys, (((1,), (1,)), ((), ())), preferred_element_type=jnp.float32
                    )
                    * scale
                )
                scores = jnp.where(alive, scores, -1e30)
                self_key = sk_ref[r : r + 1, part].astype(jnp.float32)
                self_score = (
                    jnp.sum(q.astype(jnp.float32) * self_key, axis=1, keepdims=True) * scale
                )
                top = jnp.maximum(jnp.max(scores, axis=1, keepdims=True), self_score)
                weights = jnp.where(alive, jnp.exp(scores - top), 0.0)
                self_weight = jnp.exp(self_score - top)
                total = jnp.sum(weights, axis=1, keepdims=True) + self_weight
                mixed = lax.dot_general(
                    weights.astype(jnp.bfloat16),
                    values,
                    (((1,), (0,)), ((), ())),
                    preferred_element_type=jnp.float32,
                )
                self_rounded = self_weight.astype(jnp.bfloat16).astype(jnp.float32)
                mixed = mixed + self_rounded * sv_ref[r : r + 1, part].astype(jnp.float32)
                out_ref[r, here, :] = (mixed / total).astype(jnp.bfloat16)

    return pl.pallas_call(
        kernel,
        out_shape=jax.ShapeDtypeStruct((rows, heads, HD), jnp.bfloat16),
        in_specs=[SMEM, VMEM, VMEM, VMEM, VMEM, ANY, ANY, ANY, ANY],
        out_specs=VMEM,
        scratch_shapes=[
            pltpu.VMEM((rows, k_sel, page_rows, width), jnp.bfloat16),
            pltpu.VMEM((rows, k_sel, page_rows, width), jnp.bfloat16),
            pltpu.SemaphoreType.DMA((rows, 2)),
        ],
        compiler_params=params(),
        name="attend",
    )(
        page_slots,
        live,
        queries.reshape(rows, heads, HD),
        self_keys,
        self_values,
        res_k,
        res_v,
        pool_k,
        pool_v,
    )


def project(partial):
    ranks = lax.axis_size("head")
    here = lax.axis_index("head")
    columns = partial.shape[1] // ranks

    def piece(owner):
        return lax.dynamic_slice_in_dim(partial, owner * columns, columns, 1)

    total = piece(here)
    for s in range(1, ranks):
        pairs = [(k, (k + s) % ranks) for k in range(ranks)]
        total = total + lax.ppermute(piece((here + s) % ranks), "head", pairs)
    return total.astype(jnp.bfloat16)


def on_device(
    new_keys,
    new_values,
    page_dest,
    page_slot,
    resident_keys,
    resident_values,
    queries,
    self_keys,
    self_values,
    context_len,
    selected,
    out_weight,
):
    groups = lax.axis_size("grp")
    chips = groups // CORES
    me = lax.axis_index("grp")
    chip, core = me // CORES, me % CORES
    per_source, page_rows = new_keys.shape[:2]
    res_count = resident_keys.shape[0]
    rows_here = queries.shape[0]
    pair_cap = 2 * per_source // groups
    cap = CORES * CORES * pair_cap
    unit = cap // 16
    first, second, third = 3 * unit, 4 * unit, 7 * unit // 2
    shifts = chips - 1

    def permute(x, shift):
        return lax.ppermute(x, "grp", [(i, i ^ shift) for i in range(groups)])

    def after(x, *others):
        return lax.optimization_barrier((x, *others))[0]

    def send(packed):
        return [[permute(x, (s + 1) * CORES) for s, x in enumerate(piece)] for piece in packed]

    me_list, core_list = me.reshape(1), core.reshape(1)
    own_ids = jnp.arange(per_source, dtype=jnp.int32)
    width = cap + 8

    page_counts = (context_len + page_rows - 1) // page_rows
    row_end = jnp.cumsum(page_counts)
    row_start = row_end - page_counts
    page_slots = row_start[:, None] + selected
    chosen = (page_slots.reshape(-1, 1) - res_count == own_ids[None, :]).astype(jnp.int32)
    chosen = jnp.max(chosen, axis=0)

    own_info = jnp.stack([page_dest, page_slot, chosen])
    infos = jnp.stack([own_info] + [permute(own_info, s * CORES) for s in range(1, chips)])
    infos = jnp.stack([infos, permute(infos, 1)], axis=1)
    dest, slot, flags = infos[:, :, 0], infos[:, :, 1], infos[:, :, 2]
    flags = flags.reshape(groups, per_source)

    own_sends = first_lists(me_list, page_dest[None], shifts, first)
    packed = pack_pages(
        core_list, jnp.zeros((shifts,), jnp.int32), own_sends, [first], new_keys, new_values
    )
    direct0 = send(packed)

    dest, slot = lax.optimization_barrier((dest, slot, packed))[:2]
    away = dest ^ me
    padded = -(-shifts // 8) * 8
    shift_ids = jnp.arange(1, padded + 1, dtype=jnp.int32)
    chip_away = (away[0] // CORES).reshape(1, -1)
    wanted = wanted_of(away[0], slot[0], flags).reshape(1, -1)
    ids = jnp.arange(CORES * per_source, dtype=jnp.int32)[None]
    sends, send_start = full_lists(
        (chip_away == shift_ids[:, None]).astype(jnp.int32),
        jnp.broadcast_to(wanted, (padded, wanted.shape[1])),
        jnp.broadcast_to(ids, (padded, ids.shape[1])),
        shifts,
        per_source,
        first,
        width,
    )

    new_keys_, new_values_ = lax.optimization_barrier((new_keys, new_values, packed))[:2]
    sib = (permute(new_keys_, 1), permute(new_values_, 1))

    def pack(offset, pieces, start=send_start):
        return pack_pages(core_list, start + offset, sends, pieces, new_keys, new_values, sib)

    packed = pack(0, [second])
    dest, slot = lax.optimization_barrier((dest, slot, packed))[:2]

    chip_ids = jnp.arange(chips, dtype=jnp.int32)
    counts = jnp.sum((dest[..., None] // CORES == chip_ids).astype(jnp.int32), axis=2)
    late = jnp.sum(counts, axis=1, keepdims=True) - jnp.minimum(counts, first)
    late = jnp.where((chip ^ chip_ids)[:, None, None] == chip_ids[None, None, :], 0, late)
    needed = jnp.max(late)

    def both_kinds(x):
        x = jnp.concatenate([x[1:], x[1:, ::-1]]).reshape(2 * shifts, -1)
        return padded_rows(x, -(-2 * shifts // 8) * 8)

    arrive_wanted = wanted_of(
        (dest ^ me)[1:].reshape(shifts * CORES, -1), slot[1:].reshape(shifts * CORES, -1), flags
    ).reshape(shifts, CORES, -1)
    arrive_wanted = jnp.concatenate([wanted.reshape(1, CORES, -1), arrive_wanted])
    to_chip = (dest[..., None] // CORES == chip_ids).astype(jnp.float32)
    most_wanted = jnp.max(jnp.sum(arrive_wanted[..., None] * to_chip, axis=(1, 2)))
    soon = most_wanted <= second
    arrivals, arrive_start = full_lists(
        both_kinds((dest // CORES == chip).astype(jnp.int32)),
        both_kinds(arrive_wanted),
        both_kinds((dest % CORES) * per_source + slot),
        2 * shifts,
        per_source,
        first,
        width,
    )

    packed, direct0, dest, slot, arrivals, arrive_start = lax.optimization_barrier(
        (packed, direct0, dest, slot, arrivals, arrive_start)
    )
    direct1 = send(packed)

    def spans_at(arrive_start, offset):
        start = arrive_start + offset
        return jnp.stack([start, jnp.full_like(start, width)], axis=1)

    early_spans = jnp.stack([jnp.zeros_like(arrive_start), arrive_start], axis=1)

    def settle(spans, direct, pools=()):
        swapped = [[permute(x, 1) for x in piece] for piece in direct]
        return settle_pages(core_list, spans, arrivals, direct, swapped, per_source, pools)

    slot_ids = jnp.arange(res_count + per_source, dtype=jnp.int32)
    owner_row = jnp.sum((slot_ids[None, :] >= row_end[:, None]).astype(jnp.int32), axis=0)[None]
    res_bounds = bounds_of(
        owner_row[:, :res_count], queries, after(resident_keys, packed), res_count
    )
    pools = settle(early_spans, direct0)

    locals_ = invert(
        jnp.stack([dest[0, 0] == me, dest[0, 1] == me]),
        own_ids[None, :] * per_source + slot[0],
        pair_cap,
    )

    held = [unit // 2, unit, 2 * unit, 3 * unit]
    packed, kept, direct1, pools, res_bounds, locals_ = lax.optimization_barrier(
        (
            pack(second, [third]),
            pack(second + third, held),
            direct1,
            pools,
            res_bounds,
            locals_,
        )
    )
    direct2 = send(packed)
    pools = settle_local(locals_, (new_keys, new_values), sib, pools)
    pools = settle(spans_at(arrive_start, 0), direct1, pools)

    within = jnp.arange(page_rows, dtype=jnp.int32)
    live = (
        (selected[:, :, None] * page_rows + within[None, None, :] < context_len[:, None, None])
        .astype(jnp.int32)
        .reshape(rows_here, -1)
    )

    def decode(pools):
        attended = attend(
            page_slots,
            live,
            queries,
            self_keys,
            self_values,
            resident_keys,
            resident_values,
            *pools,
        )
        return project(
            jnp.dot(attended.reshape(rows_here, -1), out_weight, preferred_element_type=jnp.float32)
        )

    projected = decode(pools)

    kept, direct2, pools, needed, soon, projected, info = lax.optimization_barrier(
        (
            kept,
            direct2,
            pools,
            needed,
            soon,
            projected,
            (send_start, arrive_start),
        )
    )

    def rest(total):
        def branch(ops):
            kept, direct, pools, (send_start, arrive_start) = ops
            arrived = []
            if total:
                arrived = send([kept[held.index(min(total, held[-1]))]])
            pools = settle(spans_at(arrive_start, second), direct, pools)
            if total > held[-1]:
                late = pack(second + third + held[-1], [total - held[-1]], send_start)
                arrived = arrived + send(late)
            pools, arrived = lax.optimization_barrier((pools, arrived))
            if arrived:
                pools = settle(spans_at(arrive_start, second + third), arrived, pools)
            return pools

        return branch

    totals = [0] + held + [held[-1] + k * unit for k in (1, 2)] + [cap - second - third]
    left = needed - second - third
    which = sum((left > total).astype(jnp.int32) for total in totals[:-1])
    ops = (kept, direct2, pools, info)
    if chips <= 4:
        pools = lax.switch(which, [rest(total) for total in totals], ops)
    else:
        pools = rest(totals[-1])(ops)
    pool_k, pool_v = pools
    projected = lax.cond(soon, lambda pools: projected, decode, pools)

    slot_bounds = bounds_of(
        owner_row[:, res_count:], queries, pool_k, min(128, per_source), res_bounds
    )
    return pool_k, pool_v, slot_bounds, projected


def solution(mesh):
    in_specs = (
        P("grp", None, "head"),
        P("grp", None, "head"),
        P("grp"),
        P("grp"),
        P("grp", None, "head"),
        P("grp", None, "head"),
        P("grp", "head"),
        P("grp", "head"),
        P("grp", "head"),
        P("grp"),
        P("grp", None),
        P("head", None),
    )
    out_specs = (P("grp", None, "head"), P("grp", None, "head"), P("head", "grp"), P("grp", "head"))
    return jax.shard_map(
        on_device, mesh=mesh, in_specs=in_specs, out_specs=out_specs, check_vma=False
    )
```
